32 devices in a mesh: dp: 16 (over z, x, core), seq: 2 (over y).
Axes of the slice: x: 2, y: 2, z: 4, core: 2. Of those that a mesh axis runs over, the one named last changes fastest.
Arguments:
- queries: bfloat16 [4096, 4096], P(('dp', 'seq')), may hold values from -48 to 48
- keys: bfloat16 [4096, 1024], P(('dp', 'seq')), may hold values from -6 to 6
- values: bfloat16 [4096, 1024], P(('dp', 'seq')), may hold values from -6 to 6
- out_grad: bfloat16 [4096, 4096], P(('dp', 'seq')), may hold values from -6 to 6
- normed: bfloat16 [4096, 4096], P(('dp', 'seq')), may hold values from -6 to 6
Outputs:
- query_grad: bfloat16 [4096, 4096], P(('dp', 'seq'))
- key_weight_grad: float32 [4096, 1024], P('dp', 'seq')
- value_weight_grad: float32 [4096, 1024], P('dp', 'seq')
The draws below stay inside these ranges and needn't reach their ends.
All inputs are finite; a program needn't handle non-finite values.
Results may differ from the reference program's by a relative error of at most 0.0055.
Values may be sent and summed in bfloat16 or wider, within the bound.
No kernel may reach another device: no remote copies, remote signals or barrier semaphores. Data moves between devices by JAX's collectives and lax.ppermute only.
A program may use at most 128 MiB of HBM per device.

```python
import math
import jax
import jax.numpy as jnp
from jax import lax

D = 4096
QH = 32
KV = 8
HD = 128
SEQ_LEN = 256
TOKENS = 4096


def shared_keys(key):
    base = jax.random.fold_in(key, 11)
    drawn = jax.random.truncated_normal(base, -6.0, 6.0, (TOKENS, KV * HD), jnp.float32)
    return drawn


def draw_keys(key, part):
    return shared_keys(key).astype(jnp.bfloat16)


def draw_queries(key, part):
    base = jax.random.fold_in(key, 23)
    drawn = jax.random.truncated_normal(base, -6.0, 6.0, (TOKENS, QH * HD), jnp.float32)
    return drawn.astype(jnp.bfloat16)


def with_spikes(array, stream_key, source, target, shards_of, factor):
    owner, partner = [(jnp.arange(array.shape[axis_at]) // (array.shape[axis_at] // shards_of)).reshape([-1 if axis == axis_at else 1 for axis in range(array.ndim)]) for axis_at in (source, target)]
    chosen = jax.random.permutation(stream_key, shards_of)[partner]
    strong = (owner == chosen) | (owner == (partner + shards_of // 2) % shards_of)
    return jnp.where(strong, factor * array, array)


def block_levels(stream_key, dims, split, smallest, high):
    factor_of = 1.0
    for dim, blocks in split:
        heights = jax.random.uniform(jax.random.fold_in(jax.random.fold_in(stream_key, 6), dim), (blocks,), jnp.float32, smallest / len(split), high / len(split))
        factor_of = factor_of * jnp.repeat(jnp.exp(heights), dims[dim] // blocks).reshape((-1,) + (1,) * (len(dims) - 1 - dim))
    return factor_of


def bell_draw(own_key, shape, spread, bound, cuts=(), dtype=jnp.bfloat16):
    level = block_levels(own_key, shape, cuts, -0.22, 0.18) if cuts else 1.0
    values = jax.random.normal(own_key, shape, jnp.float32) * spread * level
    return jnp.minimum(jnp.maximum(values, -bound), bound).astype(dtype)


def bell_draw_with(own_key, extent, deviation, limit, split, heavy, held_as=jnp.bfloat16):
    result = deviation * jax.random.normal(own_key, extent, jnp.float32)
    if split:
        result = result * block_levels(own_key, extent, split, -0.22, 0.18)
    return jnp.clip(with_spikes(result, jax.random.fold_in(own_key, 3), *heavy), -limit, limit).astype(held_as)


def setup_inputs(seed: int = 0) -> dict:
    seeds = jax.random.split(jax.random.key(seed), 6)
    queries = draw_queries(jax.random.fold_in(seeds[5], 71), 0)
    keys = draw_keys(jax.random.fold_in(seeds[5], 71), 0)
    values = bell_draw(seeds[2], (TOKENS, KV * HD), 1.0, 6.0, ((0, 32),))
    out_grad = bell_draw(seeds[3], (TOKENS, QH * HD), 1.0, 6.0, ((0, 32),))
    normed = bell_draw_with(seeds[4], (TOKENS, D), 1.0, 6.0, ((0, 32),), (0, 1, 32, 2.75))
    return {"queries": queries, "keys": keys, "values": values, "out_grad": out_grad, "normed": normed}


def unrotate(grad, position):
    half = HD // 2
    freqs = jnp.exp(-math.log(500000.0) * (2.0 * jnp.arange(half).astype(jnp.float32) / HD))
    angle = position.astype(jnp.float32)[:, None] * freqs[None, :]
    cosine = jnp.cos(angle)[:, None, :]
    sine = jnp.sin(angle)[:, None, :]
    first = grad[..., :half]
    second = grad[..., half:]
    return jnp.concatenate([first * cosine + second * sine, second * cosine - first * sine], axis=-1)

def one_sequence(carry, items):
    query_rows, key_rows, value_rows, grad_rows, normed_rows = items
    groups = QH // KV
    scale = 1.0 / math.sqrt(HD)
    qh = query_rows.reshape(SEQ_LEN, QH, HD).astype(jnp.float32)
    kh = jnp.repeat(key_rows.reshape(SEQ_LEN, KV, HD), groups, axis=1).astype(jnp.float32)
    vh = jnp.repeat(value_rows.reshape(SEQ_LEN, KV, HD), groups, axis=1).astype(jnp.float32)
    gh = grad_rows.reshape(SEQ_LEN, QH, HD).astype(jnp.float32)
    scores = jnp.einsum('qhd,khd->hqk', qh, kh) * scale
    position = jnp.arange(SEQ_LEN)
    allowed = position[None, :] <= position[:, None]
    scores = jnp.where(allowed[None], scores, -jnp.inf)
    top = lax.optimization_barrier(jnp.max(scores, axis=-1, keepdims=True))
    expo = jnp.where(allowed[None], jnp.exp(scores - top), 0.0)
    probs = expo / lax.optimization_barrier(jnp.sum(expo, axis=-1, keepdims=True))
    probs_b = lax.optimization_barrier(probs.astype(jnp.bfloat16)).astype(jnp.float32)
    value_heads = jnp.einsum('hqk,qhd->khd', probs_b, gh)
    value_grad = value_heads.reshape(SEQ_LEN, KV, groups, HD).sum(axis=2).reshape(SEQ_LEN, KV * HD).astype(jnp.bfloat16)
    prob_grad = jnp.einsum('qhd,khd->hqk', gh, vh)
    delta = lax.optimization_barrier(jnp.sum(probs * prob_grad, axis=-1, keepdims=True))
    score_grad = lax.optimization_barrier((probs * (prob_grad - delta) * scale).astype(jnp.bfloat16)).astype(jnp.float32)
    query_grad = jnp.einsum('hqk,khd->qhd', score_grad, kh).reshape(SEQ_LEN, QH * HD).astype(jnp.bfloat16)
    key_heads = jnp.einsum('hqk,qhd->khd', score_grad, qh)
    key_sum = key_heads.reshape(SEQ_LEN, KV, groups, HD).sum(axis=2)
    key_grad = unrotate(key_sum, position).reshape(SEQ_LEN, KV * HD).astype(jnp.bfloat16)
    key_total = carry[0] + jnp.dot(normed_rows.T, key_grad, preferred_element_type=jnp.float32)
    value_total = carry[1] + jnp.dot(normed_rows.T, value_grad, preferred_element_type=jnp.float32)
    return ((key_total, value_total), query_grad)

def reference(queries, keys, values, out_grad, normed):
    count = TOKENS // SEQ_LEN
    items = (queries.reshape(count, SEQ_LEN, QH * HD), keys.reshape(count, SEQ_LEN, KV * HD), values.reshape(count, SEQ_LEN, KV * HD), out_grad.reshape(count, SEQ_LEN, QH * HD), normed.reshape(count, SEQ_LEN, D))
    start = (jnp.zeros((D, KV * HD), jnp.float32), jnp.zeros((D, KV * HD), jnp.float32))
    totals, query_grad = lax.scan(one_sequence, start, items)
    return (query_grad.reshape(TOKENS, QH * HD), totals[0], totals[1])
```

```python
import math

import jax
import jax.numpy as jnp
import numpy as np
from jax import lax
from jax.experimental import pallas as pl
from jax.experimental.pallas import tpu as pltpu
from jax.sharding import PartitionSpec as P

HD = 128
NC = 2
BF = jnp.bfloat16
F32 = jnp.float32
VMEM_LIMIT = 40 * 1024 * 1024


def unrotate(grad, position):
    half = HD // 2
    freqs = jnp.exp(-math.log(500000.0) * (2.0 * jnp.arange(half).astype(jnp.float32) / HD))
    angle = position.astype(jnp.float32)[:, None] * freqs[None, :]
    cosine = jnp.cos(angle)[:, None, :]
    sine = jnp.sin(angle)[:, None, :]
    first = grad[..., :half]
    second = grad[..., half:]
    return jnp.concatenate(
        [first * cosine + second * sine, second * cosine - first * sine], axis=-1
    )


def general_local(queries, keys, values, out_grad, normed):
    head_q, head_k, head_v, head_g = (
        lax.all_to_all(queries, "seq", split_axis=1, concat_axis=0, tiled=True),
        lax.all_to_all(keys, "seq", split_axis=1, concat_axis=0, tiled=True),
        lax.all_to_all(values, "seq", split_axis=1, concat_axis=0, tiled=True),
        lax.all_to_all(out_grad, "seq", split_axis=1, concat_axis=0, tiled=True),
    )
    length = head_q.shape[0]
    heads = head_q.shape[1] // HD
    kv_heads = head_k.shape[1] // HD
    groups = heads // kv_heads
    scale = 1.0 / math.sqrt(HD)
    block = length if length <= 512 else max(512, length // 8)
    starts = list(range(0, length, block))
    query_parts = [[None] * heads for first in starts]
    key_groups = []
    value_groups = []
    for group in range(kv_heads):
        low = group * HD
        high = low + HD
        key_acc = jnp.zeros((length, HD), jnp.float32)
        value_acc = jnp.zeros((length, HD), jnp.float32)
        for number, first in enumerate(starts):
            last = first + block
            query_pos = first + jnp.arange(block)[:, None]
            key_pos = jnp.arange(last)[None, :]
            allowed = key_pos <= query_pos
            key_block = head_k[:last, low:high]
            value_block = head_v[:last, low:high]
            for member in range(groups):
                head = group * groups + member
                query_block = head_q[first:last, head * HD : (head + 1) * HD]
                grad_block = head_g[first:last, head * HD : (head + 1) * HD]
                scores = (
                    lax.dot_general(
                        query_block,
                        key_block,
                        (((1,), (1,)), ((), ())),
                        preferred_element_type=jnp.float32,
                    )
                    * scale
                )
                scores = jnp.where(allowed, scores, -jnp.inf)
                top = jnp.max(scores, axis=1, keepdims=True)
                expo = jnp.where(allowed, jnp.exp(scores - top), 0.0)
                probs = expo / jnp.sum(expo, axis=1, keepdims=True)
                probs_b = probs.astype(jnp.bfloat16)
                value_acc = value_acc.at[:last].add(
                    lax.dot_general(
                        probs_b,
                        grad_block,
                        (((0,), (0,)), ((), ())),
                        preferred_element_type=jnp.float32,
                    )
                )
                prob_grad = lax.dot_general(
                    grad_block,
                    value_block,
                    (((1,), (1,)), ((), ())),
                    preferred_element_type=jnp.float32,
                )
                delta = jnp.sum(probs * prob_grad, axis=1, keepdims=True)
                score_grad = (probs * (prob_grad - delta) * scale).astype(jnp.bfloat16)
                query_parts[number][head] = jnp.dot(
                    score_grad, key_block, preferred_element_type=jnp.float32
                ).astype(jnp.bfloat16)
                key_acc = key_acc.at[:last].add(
                    lax.dot_general(
                        score_grad,
                        query_block,
                        (((0,), (0,)), ((), ())),
                        preferred_element_type=jnp.float32,
                    )
                )
        key_groups.append(key_acc)
        value_groups.append(value_acc)
    head_query_grad = jnp.concatenate(
        [jnp.concatenate(parts, axis=1) for parts in query_parts], axis=0
    )
    rows_pos = jnp.arange(length)
    key_total = jnp.stack(key_groups, axis=1)
    key_grad = unrotate(key_total, rows_pos).reshape(length, kv_heads * HD).astype(jnp.bfloat16)
    value_grad = jnp.concatenate(value_groups, axis=1).astype(jnp.bfloat16)
    query_grad = lax.all_to_all(head_query_grad, "seq", split_axis=0, concat_axis=1, tiled=True)
    width = normed.shape[1]
    piece = lax.all_gather(normed, "seq", axis=0, tiled=True)
    key_part = lax.dot_general(
        piece, key_grad, (((0,), (0,)), ((), ())), preferred_element_type=jnp.float32
    )
    value_part = lax.dot_general(
        piece, value_grad, (((0,), (0,)), ((), ())), preferred_element_type=jnp.float32
    )
    key_full, value_full = lax.psum((key_part, value_part), "dp")
    share = width // lax.axis_size("dp")
    offset = lax.axis_index("dp") * share
    key_weight_grad = lax.dynamic_slice_in_dim(key_full, offset, share, 0)
    value_weight_grad = lax.dynamic_slice_in_dim(value_full, offset, share, 0)
    return (query_grad, key_weight_grad, value_weight_grad)


CORE, XBIT, ZLOW, ZHIGH = 1, 2, 4, 8


def flip(array, mask):
    return lax.ppermute(array, "dp", [(i, i ^ mask) for i in range(16)])


def swap_seq(array):
    return lax.ppermute(array, "seq", [(0, 1), (1, 0)])


def params():
    return pltpu.CompilerParams(vmem_limit_bytes=VMEM_LIMIT)


def rotary_tables(length):
    half = HD // 2
    freqs = np.exp(-math.log(500000.0) * (2.0 * np.arange(half, dtype=np.float64) / HD))
    angle = np.arange(length, dtype=np.float64)[:, None] * freqs[None, :]
    cosine = np.concatenate([np.cos(angle), np.cos(angle)], axis=1)
    sine = np.concatenate([np.sin(angle), -np.sin(angle)], axis=1)
    return cosine.astype(np.float32), sine.astype(np.float32)


def pack_kv(keys, values):
    rows = keys.shape[0]
    wide = keys.shape[1] // (2 * NC)

    def body(k_ref, v_ref, *outs):
        for chunk, out in enumerate(outs):
            for number, ref in enumerate((k_ref, v_ref)):
                for half in range(2):
                    low = (half * NC + chunk) * wide
                    at = (number * 2 + half) * wide
                    out[:, at : at + wide] = ref[:, low : low + wide]

    return pl.pallas_call(
        body,
        out_shape=[jax.ShapeDtypeStruct((rows, 4 * wide), BF)] * NC,
        compiler_params=params(),
        name="pack_kv",
    )(keys, values)


def split_normed(normed, me):
    rows, width = normed.shape
    share = width // 16

    def body(me_ref, x_ref, same_ref, other_ref):
        mine = me_ref[0]
        for core, out in enumerate((same_ref, other_ref)):
            for place in range(8):
                zlow, xbit, zhigh = place >> 2, (place >> 1) & 1, place & 1
                mask = zhigh * ZHIGH + zlow * ZLOW + xbit * XBIT + core
                low = pl.multiple_of((mine ^ mask) * share, share)
                out[:, place * share : (place + 1) * share] = x_ref[:, pl.ds(low, share)]

    vmem = pl.BlockSpec(memory_space=pltpu.VMEM)
    return pl.pallas_call(
        body,
        out_shape=[jax.ShapeDtypeStruct((rows, width // 2), BF)] * 2,
        in_specs=[pl.BlockSpec(memory_space=pltpu.SMEM), vmem],
        out_specs=[vmem, vmem],
        compiler_params=params(),
        name="split_normed",
    )(me, normed)


def pack_normed(same, recv):
    rows, width = same.shape
    wide = width // 4

    def body(a_ref, b_ref, *outs):
        for place, out in enumerate(outs):
            out[:rows, :] = a_ref[:, place * wide : (place + 1) * wide]
            out[rows:, :] = b_ref[:, place * wide : (place + 1) * wide]

    return pl.pallas_call(
        body,
        out_shape=[jax.ShapeDtypeStruct((2 * rows, wide), BF)] * 4,
        compiler_params=params(),
        name="pack_normed",
    )(same, recv)


def attention(chunk, seq_at, queries, out_grad, keys, values, kv_recv, cosine, sine, grad_so_far):
    rows, width = queries.shape
    wide = width // (2 * NC)
    kv_wide = keys.shape[1] // (2 * NC)
    kv_heads = kv_wide // HD
    groups = wide // kv_wide
    span = groups * rows
    scale = 1.0 / math.sqrt(HD)

    def rotate(grad, cos, sin):
        return grad * cos + pltpu.roll(grad, HD // 2, 1) * sin

    def nt(a, b):
        return lax.dot_general(a, b, (((1,), (1,)), ((), ())), preferred_element_type=F32)

    def tn(a, b):
        return lax.dot_general(a, b, (((0,), (0,)), ((), ())), preferred_element_type=F32)

    def body(at_ref, q_ref, g_ref, k_ref, v_ref, ko_ref, vo_ref, cos_ref, sin_ref, *rest):
        qg_ref, keep_a, keep_b, send = rest[-4:]
        other = pl.program_id(0)
        late = at_ref[0]

        def stack(ref, head):
            return jnp.concatenate(
                [
                    ref[:, (head * groups + m) * HD : (head * groups + m + 1) * HD]
                    for m in range(groups)
                ],
                axis=0,
            )

        def one_head(head, is_late):
            cols = slice(head * HD, (head + 1) * HD)
            qs = stack(q_ref, head)
            gs = stack(g_ref, head)
            ks = k_ref[:, cols]
            vs = v_ref[:, cols]
            if is_late:
                ks = jnp.concatenate([ko_ref[:, cols], ks], axis=0)
                vs = jnp.concatenate([vo_ref[:, cols], vs], axis=0)
            count = ks.shape[0]
            scores = nt(ks, qs) * scale
            key_pos = lax.broadcasted_iota(jnp.int32, (count, span), 0) - (count - rows)
            query_pos = lax.broadcasted_iota(jnp.int32, (count, span), 1) % rows
            scores = jnp.where(key_pos <= query_pos, scores, -1e30)
            top = jnp.max(scores, axis=0, keepdims=True)
            expo = jnp.exp(scores - top)
            probs = expo * (1.0 / jnp.sum(expo, axis=0, keepdims=True))
            value_grad = jnp.dot(probs.astype(BF), gs, preferred_element_type=F32)
            prob_grad = nt(vs, gs)
            delta = jnp.sum(probs * prob_grad, axis=0, keepdims=True)
            score_grad = (probs * (prob_grad - delta) * scale).astype(BF)
            key_grad = jnp.dot(score_grad, qs, preferred_element_type=F32)
            query_grad = tn(score_grad, ks).astype(BF)
            for m in range(groups):
                low = (head * groups + m) * HD
                qg_ref[:, low : low + HD] = query_grad[m * rows : (m + 1) * rows]
            first = (rotate(key_grad[:rows], cos_ref[:rows], sin_ref[:rows]), value_grad[:rows])
            second = None
            if is_late:
                second = (
                    rotate(key_grad[rows:], cos_ref[rows:], sin_ref[rows:]),
                    value_grad[rows:],
                )
            return first, second

        def all_heads(is_late):
            parts = [one_head(head, is_late) for head in range(kv_heads)]

            def write(first_ref, second_ref, second_at):
                for head, (first, second) in enumerate(parts):
                    for number in range(2):
                        at = slice(number * kv_wide + head * HD, number * kv_wide + (head + 1) * HD)
                        first_ref[:rows, at] = first[number].astype(first_ref.dtype)
                        later = jnp.zeros((rows, HD), BF) if second is None else second[number].astype(BF)
                        second_ref[second_at : second_at + rows, at] = later

            @pl.when(other == 0)
            def _():
                write(keep_a, keep_b, 0)

            @pl.when(other == 1)
            def _():
                write(send, send, rows)

        @pl.when(late == 1)
        def _():
            all_heads(True)

        @pl.when(late == 0)
        def _():
            all_heads(False)

    def block(j, at):
        return (at[0] ^ j) * NC + chunk

    whole = lambda j, at: (0, 0)
    mine = lambda j, at: (0, block(j, at))
    specs = [
        pl.BlockSpec((rows, wide), mine),
        pl.BlockSpec((rows, wide), mine),
        pl.BlockSpec((rows, kv_wide), mine),
        pl.BlockSpec((rows, kv_wide), mine),
        pl.BlockSpec((rows, kv_wide), lambda j, at: (0, at[0] ^ j)),
        pl.BlockSpec((rows, kv_wide), lambda j, at: (0, 2 + (at[0] ^ j))),
        pl.BlockSpec((2 * rows, HD), whole),
        pl.BlockSpec((2 * rows, HD), whole),
    ]
    operands = [queries, out_grad, keys, values, kv_recv, kv_recv, cosine, sine]
    aliases = {}
    if grad_so_far is not None:
        specs.append(pl.BlockSpec(memory_space=pl.ANY))
        operands.append(grad_so_far)
        aliases = {9: 0}
    return pl.pallas_call(
        body,
        out_shape=[
            jax.ShapeDtypeStruct((rows, width), BF),
            jax.ShapeDtypeStruct((rows, 2 * kv_wide), F32),
            jax.ShapeDtypeStruct((rows, 2 * kv_wide), BF),
            jax.ShapeDtypeStruct((2 * rows, 2 * kv_wide), BF),
        ],
        grid_spec=pltpu.PrefetchScalarGridSpec(
            num_scalar_prefetch=1,
            grid=(2,),
            in_specs=specs,
            out_specs=[
                pl.BlockSpec((rows, wide), mine),
                pl.BlockSpec((rows, 2 * kv_wide), whole),
                pl.BlockSpec((rows, 2 * kv_wide), whole),
                pl.BlockSpec((2 * rows, 2 * kv_wide), whole),
            ],
        ),
        input_output_aliases=aliases,
        compiler_params=params(),
        name="attention",
    )(seq_at, *operands)


def project(normed_parts, grads):
    rows = grads[0].shape[0] // 2
    wide = grads[0].shape[1]
    share = normed_parts[0].shape[1] // 2

    def body(*refs):
        xs, ys = refs[:8], refs[8:16]
        keep, send = refs[16:]
        left = jnp.concatenate([ref[...] for ref in xs], axis=0)
        right = jnp.concatenate(
            [
                ys[place * 2 + core][seq * rows : (seq + 1) * rows, :]
                for place in range(4)
                for seq in range(2)
                for core in range(2)
            ],
            axis=0,
        )
        total = lax.dot_general(
            left, right, (((0,), (0,)), ((), ())), preferred_element_type=F32
        )
        keep[...] = total[:share]
        send[...] = total[share:].astype(BF)

    return pl.pallas_call(
        body,
        out_shape=[
            jax.ShapeDtypeStruct((share, wide), F32),
            jax.ShapeDtypeStruct((share, wide), BF),
        ],
        compiler_params=params(),
        name="project",
    )(*normed_parts, *grads)


def cube_local(queries, keys, values, out_grad, normed):
    seq = lax.axis_index("seq")
    seq_at = jnp.reshape(seq, (1,)).astype(jnp.int32)
    me = jnp.reshape(lax.axis_index("dp"), (1,)).astype(jnp.int32)
    rows = queries.shape[0]
    cosine, sine = (jnp.asarray(table) for table in rotary_tables(2 * rows))

    kv_recv = [lax.ppermute(part, "seq", [(0, 1)]) for part in pack_kv(keys, values)]
    same, other = split_normed(normed, me)
    places = pack_normed(same, flip(other, CORE))
    places = [places[0]] + [flip(places[n], mask) for n, mask in ((1, XBIT), (2, ZLOW), (3, XBIT | ZLOW))]

    query_grad = None
    kept, sent = [], []
    normed_parts = None
    for chunk in range(NC):
        query_grad, keep_a, keep_b, send = attention(
            chunk, seq_at, queries, out_grad, keys, values, kv_recv[chunk], cosine, sine, query_grad
        )
        recv = swap_seq(send)
        early = (keep_a + recv[:rows].astype(F32)).astype(BF)
        later = jnp.where(seq == 1, keep_b, recv[rows:])
        mine = jnp.concatenate(
            [jnp.where(seq == 1, later, early), jnp.where(seq == 1, early, later)], axis=0
        )
        gathered = [mine] + [flip(mine, mask) for mask in (XBIT, ZLOW, XBIT | ZLOW)]
        grads = [part for one in gathered for part in (one, flip(one, CORE))]
        if normed_parts is None:
            normed_parts = [part for one in places for part in (one, swap_seq(one))]
        keep, send = project(normed_parts, grads)
        kept.append(keep)
        sent.append(flip(send, ZHIGH))
    totals = [keep + recv.astype(F32) for keep, recv in zip(kept, sent)]
    half = totals[0].shape[1] // 2
    key_weight_grad = jnp.concatenate([one[:, :half] for one in totals], axis=1)
    value_weight_grad = jnp.concatenate([one[:, half:] for one in totals], axis=1)
    return (query_grad, key_weight_grad, value_weight_grad)


def solution(mesh):
    spread = P(("dp", "seq"), None)
    cube = dict(mesh.shape) == {"dp": 16, "seq": 2}
    return jax.shard_map(
        cube_local if cube else general_local,
        mesh=mesh,
        in_specs=(spread,) * 5,
        out_specs=(spread, P("dp", "seq"), P("dp", "seq")),
        check_vma=False,
    )
```

```python
import math

import jax
import jax.numpy as jnp
import numpy as np
from jax import lax
from jax.experimental import pallas as pl
from jax.experimental.pallas import tpu as pltpu
from jax.sharding import PartitionSpec as P

HD = 128
NC = 2
BF = jnp.bfloat16
F32 = jnp.float32
VMEM_LIMIT = 20 * 1024 * 1024
VMEM_FULL = 60 * 1024 * 1024


def unrotate(grad, position):
    half = HD // 2
    freqs = jnp.exp(-math.log(500000.0) * (2.0 * jnp.arange(half).astype(jnp.float32) / HD))
    angle = position.astype(jnp.float32)[:, None] * freqs[None, :]
    cosine = jnp.cos(angle)[:, None, :]
    sine = jnp.sin(angle)[:, None, :]
    first = grad[..., :half]
    second = grad[..., half:]
    return jnp.concatenate(
        [first * cosine + second * sine, second * cosine - first * sine], axis=-1
    )


def general_local(queries, keys, values, out_grad, normed):
    head_q, head_k, head_v, head_g = (
        lax.all_to_all(queries, "seq", split_axis=1, concat_axis=0, tiled=True),
        lax.all_to_all(keys, "seq", split_axis=1, concat_axis=0, tiled=True),
        lax.all_to_all(values, "seq", split_axis=1, concat_axis=0, tiled=True),
        lax.all_to_all(out_grad, "seq", split_axis=1, concat_axis=0, tiled=True),
    )
    length = head_q.shape[0]
    heads = head_q.shape[1] // HD
    kv_heads = head_k.shape[1] // HD
    groups = heads // kv_heads
    scale = 1.0 / math.sqrt(HD)
    block = length if length <= 512 else max(512, length // 8)
    starts = list(range(0, length, block))
    query_parts = [[None] * heads for first in starts]
    key_groups = []
    value_groups = []
    for group in range(kv_heads):
        low = group * HD
        high = low + HD
        key_acc = jnp.zeros((length, HD), jnp.float32)
        value_acc = jnp.zeros((length, HD), jnp.float32)
        for number, first in enumerate(starts):
            last = first + block
            query_pos = first + jnp.arange(block)[:, None]
            key_pos = jnp.arange(last)[None, :]
            allowed = key_pos <= query_pos
            key_block = head_k[:last, low:high]
            value_block = head_v[:last, low:high]
            for member in range(groups):
                head = group * groups + member
                query_block = head_q[first:last, head * HD : (head + 1) * HD]
                grad_block = head_g[first:last, head * HD : (head + 1) * HD]
                scores = (
                    lax.dot_general(
                        query_block,
                        key_block,
                        (((1,), (1,)), ((), ())),
                        preferred_element_type=jnp.float32,
                    )
                    * scale
                )
                scores = jnp.where(allowed, scores, -jnp.inf)
                top = jnp.max(scores, axis=1, keepdims=True)
                expo = jnp.where(allowed, jnp.exp(scores - top), 0.0)
                probs = expo / jnp.sum(expo, axis=1, keepdims=True)
                probs_b = probs.astype(jnp.bfloat16)
                value_acc = value_acc.at[:last].add(
                    lax.dot_general(
                        probs_b,
                        grad_block,
                        (((0,), (0,)), ((), ())),
                        preferred_element_type=jnp.float32,
                    )
                )
                prob_grad = lax.dot_general(
                    grad_block,
                    value_block,
                    (((1,), (1,)), ((), ())),
                    preferred_element_type=jnp.float32,
                )
                delta = jnp.sum(probs * prob_grad, axis=1, keepdims=True)
                score_grad = (probs * (prob_grad - delta) * scale).astype(jnp.bfloat16)
                query_parts[number][head] = jnp.dot(
                    score_grad, key_block, preferred_element_type=jnp.float32
                ).astype(jnp.bfloat16)
                key_acc = key_acc.at[:last].add(
                    lax.dot_general(
                        score_grad,
                        query_block,
                        (((0,), (0,)), ((), ())),
                        preferred_element_type=jnp.float32,
                    )
                )
        key_groups.append(key_acc)
        value_groups.append(value_acc)
    head_query_grad = jnp.concatenate(
        [jnp.concatenate(parts, axis=1) for parts in query_parts], axis=0
    )
    rows_pos = jnp.arange(length)
    key_total = jnp.stack(key_groups, axis=1)
    key_grad = unrotate(key_total, rows_pos).reshape(length, kv_heads * HD).astype(jnp.bfloat16)
    value_grad = jnp.concatenate(value_groups, axis=1).astype(jnp.bfloat16)
    query_grad = lax.all_to_all(head_query_grad, "seq", split_axis=0, concat_axis=1, tiled=True)
    width = normed.shape[1]
    piece = lax.all_gather(normed, "seq", axis=0, tiled=True)
    key_part = lax.dot_general(
        piece, key_grad, (((0,), (0,)), ((), ())), preferred_element_type=jnp.float32
    )
    value_part = lax.dot_general(
        piece, value_grad, (((0,), (0,)), ((), ())), preferred_element_type=jnp.float32
    )
    key_full, value_full = lax.psum((key_part, value_part), "dp")
    share = width // lax.axis_size("dp")
    offset = lax.axis_index("dp") * share
    key_weight_grad = lax.dynamic_slice_in_dim(key_full, offset, share, 0)
    value_weight_grad = lax.dynamic_slice_in_dim(value_full, offset, share, 0)
    return (query_grad, key_weight_grad, value_weight_grad)


CORE, XBIT, ZLOW, ZHIGH = 1, 2, 4, 8


def flip(array, mask):
    return lax.ppermute(array, "dp", [(i, i ^ mask) for i in range(16)])


def swap_seq(array):
    return lax.ppermute(array, "seq", [(0, 1), (1, 0)])


def params(limit=VMEM_LIMIT):
    return pltpu.CompilerParams(vmem_limit_bytes=limit)


def vmem():
    return pl.BlockSpec(memory_space=pltpu.VMEM)


def smem():
    return pl.BlockSpec(memory_space=pltpu.SMEM)


def rotary_tables(length):
    half = HD // 2
    freqs = np.exp(-math.log(500000.0) * (2.0 * np.arange(half, dtype=np.float64) / HD))
    angle = np.arange(length, dtype=np.float64)[:, None] * freqs[None, :]
    cosine = np.concatenate([np.cos(angle), np.cos(angle)], axis=1)
    sine = np.concatenate([np.sin(angle), -np.sin(angle)], axis=1)
    return cosine.astype(np.float32), sine.astype(np.float32)


def hbm():
    return pl.BlockSpec(memory_space=pltpu.HBM)


def in_hbm(array):
    return pltpu.with_memory_space_constraint(array, pltpu.HBM)


def run_copies(copies):
    for copy in copies:
        copy.start()
    for copy in copies:
        copy.wait()


def prepare(keys, values, normed, me):
    rows, kv_width = keys.shape
    width = normed.shape[1]
    share = width // 16
    wide = kv_width // (2 * NC)

    def body(me_ref, k_hbm, v_hbm, x_hbm, k_ref, v_ref, *rest):
        kv, parts, (x_ref, sem) = rest[:NC], rest[NC : NC + 4], rest[NC + 4 :]
        mine = me_ref[0]
        run_copies(
            [
                pltpu.make_async_copy(k_hbm, k_ref, sem.at[0]),
                pltpu.make_async_copy(v_hbm, v_ref, sem.at[1]),
                pltpu.make_async_copy(x_hbm, x_ref, sem.at[2]),
            ]
        )
        for chunk, out in enumerate(kv):
            for number, ref in enumerate((k_ref, v_ref)):
                for half in range(2):
                    low = (half * NC + chunk) * wide
                    at = (number * 2 + half) * wide
                    out[:, at : at + wide] = ref[:, low : low + wide]

        for place, part in enumerate(parts):
            for number, mask in enumerate((ZHIGH, ZHIGH | CORE, 0, CORE)):
                low = pl.multiple_of((mine ^ (mask | (place * 2))) * share, share)
                part[number] = x_ref[:, pl.ds(low, share)]

    return pl.pallas_call(
        body,
        out_shape=[pltpu.VMEM((rows, kv_width), BF)] * 2
        + [pltpu.VMEM((rows, 4 * wide), BF)] * NC
        + [pltpu.VMEM((4, rows, share), BF)] * 4,
        in_specs=[smem()] + [hbm()] * 3,
        out_specs=[vmem()] * (6 + NC),
        scratch_shapes=[pltpu.VMEM((rows, width), BF), pltpu.SemaphoreType.DMA((3,))],
        compiler_params=params(),
        name="prepare",
    )(me, in_hbm(keys), in_hbm(values), in_hbm(normed))


def stage(arrays):
    count = len(arrays)

    def body(*refs):
        run_copies(
            [
                pltpu.make_async_copy(refs[n], refs[count + n], refs[-1].at[n])
                for n in range(count)
            ]
        )

    return pl.pallas_call(
        body,
        out_shape=[pltpu.VMEM(one.shape, one.dtype) for one in arrays],
        in_specs=[hbm()] * count,
        out_specs=[vmem()] * count,
        scratch_shapes=[pltpu.SemaphoreType.DMA((count,))],
        compiler_params=params(),
        name="stage",
    )(*[in_hbm(one) for one in arrays])


def pack_normed(parts, numbers, after):
    rows, share = parts[0].shape[1:]
    shapes = [(4,) + (len(group),) * (len(group) > 1) + (rows, share) for group in numbers]

    def body(*refs):
        for group, out in zip(numbers, refs[-len(numbers) :]):
            for place in range(4):
                if len(group) > 1:
                    for at, number in enumerate(group):
                        out[place, at] = refs[place][number]
                else:
                    out[place] = refs[place][group[0]]

    return pl.pallas_call(
        body,
        out_shape=[pltpu.VMEM(shape, BF) for shape in shapes],
        in_specs=[vmem()] * 4 + [hbm()] * len(after),
        out_specs=[vmem()] * len(shapes),
        compiler_params=params(),
        name="pack_normed",
    )(*parts, *after)


def combine(seq_at, keep_a, keep_b, recv, after):
    rows, wide = keep_a.shape

    def body(at_ref, a_ref, b_ref, recv_ref, *rest):
        out = rest[-1]
        early = (a_ref[...] + recv_ref[:rows].astype(F32)).astype(BF)

        @pl.when(at_ref[0] == 0)
        def _():
            out[:rows] = early
            out[rows:] = recv_ref[rows:]

        @pl.when(at_ref[0] == 1)
        def _():
            out[:rows] = b_ref[...]
            out[rows:] = early

    return pl.pallas_call(
        body,
        out_shape=jax.ShapeDtypeStruct((2 * rows, wide), BF),
        in_specs=[smem(), vmem(), vmem(), vmem()] + [hbm()] * len(after),
        out_specs=vmem(),
        compiler_params=params(),
        name="combine",
    )(seq_at, keep_a, keep_b, recv, *after)


def attention(
    chunk, seq_at, queries, out_grad, keys, values, kv_recv, cosine, sine, grad_so_far, after
):
    rows, width = queries.shape
    wide = width // (2 * NC)
    kv_wide = keys.shape[1] // (2 * NC)
    kv_heads = kv_wide // HD
    groups = wide // kv_wide
    span = groups * rows
    scale = 1.0 / math.sqrt(HD)

    def rotate(grad, cos, sin):
        return grad * cos + pltpu.roll(grad, HD // 2, 1) * sin

    def nt(a, b):
        return lax.dot_general(a, b, (((1,), (1,)), ((), ())), preferred_element_type=F32)

    def tn(a, b):
        return lax.dot_general(a, b, (((0,), (0,)), ((), ())), preferred_element_type=F32)

    def body(at_ref, q_ref, g_ref, k_ref, v_ref, kv_ref, cos_ref, sin_ref, *rest):
        qg_hbm, keep_a, keep_b, send, qg_buf, out_sem = rest[-6:]
        late = at_ref[0]

        def columns(j, size):
            return pl.ds(pl.multiple_of(((late ^ j) * NC + chunk) * size, size), size)

        outs = [
            pltpu.make_async_copy(qg_buf.at[j], qg_hbm.at[:, columns(j, wide)], out_sem.at[j])
            for j in range(2)
        ]
        for j in (1, 0):
            one_side(
                j, late,
                q_ref.at[:, columns(j, wide)], g_ref.at[:, columns(j, wide)],
                k_ref.at[:, columns(j, kv_wide)], v_ref.at[:, columns(j, kv_wide)],
                kv_ref, cos_ref, sin_ref, qg_buf.at[j], keep_a, keep_b, send,
            )
            outs[j].start()
        for copy in outs:
            copy.wait()

    def one_side(
        other, late, q_ref, g_ref, k_ref, v_ref, kv_ref, cos_ref, sin_ref, qg_ref, keep_a, keep_b, send
    ):
        def earlier(number, head):
            low = (number * 2 + (late ^ other)) * kv_wide + head * HD
            return kv_ref[:, pl.ds(pl.multiple_of(low, HD), HD)]

        def stack(ref, head):
            return jnp.concatenate(
                [
                    ref[:, (head * groups + m) * HD : (head * groups + m + 1) * HD]
                    for m in range(groups)
                ],
                axis=0,
            )

        def one_head(head, is_late):
            cols = slice(head * HD, (head + 1) * HD)
            qs = stack(q_ref, head)
            gs = stack(g_ref, head)
            ks = k_ref[:, cols]
            vs = v_ref[:, cols]
            if is_late:
                ks = jnp.concatenate([earlier(0, head), ks], axis=0)
                vs = jnp.concatenate([earlier(1, head), vs], axis=0)
            count = ks.shape[0]
            scores = nt(ks, qs)
            key_pos = lax.broadcasted_iota(jnp.int32, (rows, span), 0)
            query_pos = lax.broadcasted_iota(jnp.int32, (rows, span), 1) % rows
            diagonal = jnp.where(key_pos <= query_pos, scores[count - rows :], -1e30)
            scores = jnp.concatenate([scores[:rows], diagonal], axis=0) if is_late else diagonal
            top = jnp.max(scores, axis=0, keepdims=True)
            expo = jnp.exp2((scores - top) * (scale / math.log(2.0)))
            probs = expo * (1.0 / jnp.sum(expo, axis=0, keepdims=True))
            value_grad = jnp.dot(probs.astype(BF), gs, preferred_element_type=F32)
            prob_grad = nt(vs, gs)
            delta = jnp.sum(probs * prob_grad, axis=0, keepdims=True)
            score_grad = (probs * (prob_grad - delta) * scale).astype(BF)
            key_grad = jnp.dot(score_grad, qs, preferred_element_type=F32)
            query_grad = tn(score_grad, ks).astype(BF)
            for m in range(groups):
                low = (head * groups + m) * HD
                qg_ref[:, low : low + HD] = query_grad[m * rows : (m + 1) * rows]
            first = (rotate(key_grad[:rows], cos_ref[:rows], sin_ref[:rows]), value_grad[:rows])
            second = None
            if is_late:
                second = (
                    rotate(key_grad[rows:], cos_ref[rows:], sin_ref[rows:]),
                    value_grad[rows:],
                )
            return first, second

        def all_heads(is_late):
            parts = [one_head(head, is_late) for head in range(kv_heads)]

            def write(first_ref, second_ref, second_at):
                for head, (first, second) in enumerate(parts):
                    for number in range(2):
                        at = slice(number * kv_wide + head * HD, number * kv_wide + (head + 1) * HD)
                        first_ref[:rows, at] = first[number].astype(first_ref.dtype)
                        later = jnp.zeros((rows, HD), BF) if second is None else second[number].astype(BF)
                        second_ref[second_at : second_at + rows, at] = later

            if other == 0:
                write(keep_a, keep_b, 0)
            else:
                write(send, send, rows)

        @pl.when(late == 1)
        def _():
            all_heads(True)

        @pl.when(late == 0)
        def _():
            all_heads(False)

    operands = [seq_at, queries, out_grad, keys, values, kv_recv, cosine, sine]
    specs = [smem()] + [vmem()] * 7
    aliases = {}
    if grad_so_far is not None:
        specs.append(hbm())
        operands.append(grad_so_far)
        aliases = {8: 0}
    specs += [hbm()] * len(after)
    operands += after
    return pl.pallas_call(
        body,
        out_shape=[
            jax.ShapeDtypeStruct((rows, width), BF),
            pltpu.VMEM((rows, 2 * kv_wide), F32),
            pltpu.VMEM((rows, 2 * kv_wide), BF),
            pltpu.VMEM((2 * rows, 2 * kv_wide), BF),
        ],
        in_specs=specs,
        out_specs=[hbm(), vmem(), vmem(), vmem()],
        scratch_shapes=[
            pltpu.VMEM((2, rows, wide), BF),
            pltpu.SemaphoreType.DMA((2,)),
        ],
        input_output_aliases=aliases,
        compiler_params=params(),
        name="attention",
    )(*operands)


def tn(a, b):
    return lax.dot_general(a, b, (((0,), (0,)), ((), ())), preferred_element_type=F32)


def project_away(normed_own, normed_other, grads, after):
    share = normed_own.shape[3]
    wide = grads[0].shape[1]

    def body(xa_ref, xb_ref, *refs):
        ys, outs = refs[:4], refs[-2:]
        right = jnp.concatenate([ref[...] for ref in ys], axis=0)
        for core, out in enumerate(outs):
            left = [x_ref[place, core] for place in range(4) for x_ref in (xa_ref, xb_ref)]
            out[...] = tn(jnp.concatenate(left, axis=0), right)

    return pl.pallas_call(
        body,
        out_shape=[pltpu.VMEM((share, wide), F32)] * 2,
        in_specs=[vmem()] * 6 + [hbm()] * len(after),
        out_specs=[vmem()] * 2,
        compiler_params=params(),
        name="project_away",
    )(normed_own, normed_other, *grads, *after)


def add_round(own, recv):
    def body(a_ref, b_ref, out):
        out[...] = (a_ref[...] + b_ref[...]).astype(BF)

    return pl.pallas_call(
        body,
        out_shape=pltpu.VMEM(own.shape, BF),
        in_specs=[vmem()] * 2,
        out_specs=vmem(),
        compiler_params=params(),
        name="add_round",
    )(own, recv)


def project_home(normed, grads, after):
    rows, share = normed[0].shape[1:]
    wide = grads[0][0].shape[1]
    chunks = len(grads)

    def body(*refs):
        xs, ys, out = refs[:4], refs[4 : 4 + 8 * chunks], refs[-1]
        left = [x_ref[place] for place in range(4) for x_ref in xs]
        left = jnp.concatenate(left, axis=0)
        for chunk in range(chunks):
            right = [
                ys[chunk * 8 + place * 2 + core][seq * rows : (seq + 1) * rows, :]
                for place in range(4)
                for seq in range(2)
                for core in range(2)
            ]
            out[:, chunk * wide : (chunk + 1) * wide] = tn(left, jnp.concatenate(right, axis=0))

    return pl.pallas_call(
        body,
        out_shape=pltpu.VMEM((share, chunks * wide), F32),
        in_specs=[vmem()] * (4 + 8 * chunks) + [hbm()] * len(after),
        out_specs=vmem(),
        compiler_params=params(),
        name="project_home",
    )(*normed, *[part for parts in grads for part in parts], *after)


def finish(keep, recv_half):
    rows, width = keep.shape
    wide = width // NC
    part = wide // 2

    def body(keep_ref, *refs):
        halves, outs = refs[:NC], refs[NC:]
        for chunk, half_ref in enumerate(halves):
            for number, out in enumerate(outs):
                low = number * part
                at = slice(chunk * wide + low, chunk * wide + low + part)
                out[:, chunk * part : (chunk + 1) * part] = (
                    keep_ref[:, at] + half_ref[:, low : low + part].astype(F32)
                )

    return pl.pallas_call(
        body,
        out_shape=[jax.ShapeDtypeStruct((rows, width // 2), F32)] * 2,
        in_specs=[vmem()] * (1 + NC),
        out_specs=[vmem()] * 2,
        compiler_params=params(),
        name="finish",
    )(keep, *recv_half)


def cube_local(queries, keys, values, out_grad, normed):
    seq_at = jnp.reshape(lax.axis_index("seq"), (1,)).astype(jnp.int32)
    me = jnp.reshape(lax.axis_index("dp"), (1,)).astype(jnp.int32)
    rows = queries.shape[0]
    cosine, sine = (jnp.asarray(table) for table in rotary_tables(2 * rows))

    keys, values, *rest = prepare(keys, values, normed, me)
    kv, parts = rest[:NC], rest[NC:]
    kv_recv = [lax.ppermute(part, "seq", [(0, 1)]) for part in kv]
    masks = (0, XBIT, ZLOW, XBIT | ZLOW)
    parts = [flip(part, mask) if mask else part for part, mask in zip(parts, masks)]
    q_in, g_in, cosine, sine = stage([queries, out_grad, cosine, sine])

    query_grad = None
    made = []
    for chunk in range(NC):
        query_grad, *rest = attention(
            chunk, seq_at, q_in, g_in, keys, values, kv_recv[chunk], cosine, sine, query_grad,
            parts[1:] if chunk else [],
        )
        made.append(rest)
    grads, mines = [], []
    after = [made[-1][0]]
    for keep_a, keep_b, send in made:
        mine = combine(seq_at, keep_a, keep_b, swap_seq(send), after)
        mines.append(mine)
        below = flip(mine, ZLOW)
        grads.append([mine, flip(mine, XBIT), below, flip(below, XBIT)])
        after = [grads[-1][1]]
    (away,) = pack_normed(parts, [(0, 1)], [made[-1][0]])
    away_other = swap_seq(away)
    same, cross = pack_normed(parts, [(2,), (3,)], [away_other])
    same_other, cross_other = swap_seq(same), swap_seq(cross)
    home = [same, flip(cross, CORE), same_other, flip(cross_other, CORE)]
    recv_half = []
    after = grads[1][1:3]
    for part in grads:
        own, send = project_away(away, away_other, part, after)
        total = add_round(own, flip(send, CORE))
        recv_half.append(flip(total, ZHIGH))
        after = [recv_half[-1], same_other, cross_other]
    both = [[one for one in part for one in (one, flip(one, CORE))] for part in grads]
    keep = project_home(home, both, [total])
    key_weight_grad, value_weight_grad = finish(keep, recv_half)
    return (query_grad, key_weight_grad, value_weight_grad)


def solution(mesh):
    spread = P(("dp", "seq"), None)
    cube = dict(mesh.shape) == {"dp": 16, "seq": 2}
    return jax.shard_map(
        cube_local if cube else general_local,
        mesh=mesh,
        in_specs=(spread,) * 5,
        out_specs=(spread, P("dp", "seq"), P("dp", "seq")),
        check_vma=False,
    )
```

```python
import math

import jax
import jax.numpy as jnp
import numpy as np
from jax import lax
from jax.experimental import pallas as pl
from jax.experimental.pallas import tpu as pltpu
from jax.sharding import PartitionSpec as P

HD = 128
NC = 2
BF = jnp.bfloat16
F32 = jnp.float32
VMEM_LIMIT = 20 * 1024 * 1024
CUT = 4


def unrotate(grad, position):
    half = HD // 2
    freqs = jnp.exp(-math.log(500000.0) * (2.0 * jnp.arange(half).astype(jnp.float32) / HD))
    angle = position.astype(jnp.float32)[:, None] * freqs[None, :]
    cosine = jnp.cos(angle)[:, None, :]
    sine = jnp.sin(angle)[:, None, :]
    first = grad[..., :half]
    second = grad[..., half:]
    return jnp.concatenate(
        [first * cosine + second * sine, second * cosine - first * sine], axis=-1
    )


def general_local(queries, keys, values, out_grad, normed):
    head_q, head_k, head_v, head_g = (
        lax.all_to_all(queries, "seq", split_axis=1, concat_axis=0, tiled=True),
        lax.all_to_all(keys, "seq", split_axis=1, concat_axis=0, tiled=True),
        lax.all_to_all(values, "seq", split_axis=1, concat_axis=0, tiled=True),
        lax.all_to_all(out_grad, "seq", split_axis=1, concat_axis=0, tiled=True),
    )
    length = head_q.shape[0]
    heads = head_q.shape[1] // HD
    kv_heads = head_k.shape[1] // HD
    groups = heads // kv_heads
    scale = 1.0 / math.sqrt(HD)
    block = length if length <= 512 else max(512, length // 8)
    starts = list(range(0, length, block))
    query_parts = [[None] * heads for first in starts]
    key_groups = []
    value_groups = []
    for group in range(kv_heads):
        low = group * HD
        high = low + HD
        key_acc = jnp.zeros((length, HD), jnp.float32)
        value_acc = jnp.zeros((length, HD), jnp.float32)
        for number, first in enumerate(starts):
            last = first + block
            query_pos = first + jnp.arange(block)[:, None]
            key_pos = jnp.arange(last)[None, :]
            allowed = key_pos <= query_pos
            key_block = head_k[:last, low:high]
            value_block = head_v[:last, low:high]
            for member in range(groups):
                head = group * groups + member
                query_block = head_q[first:last, head * HD : (head + 1) * HD]
                grad_block = head_g[first:last, head * HD : (head + 1) * HD]
                scores = (
                    lax.dot_general(
                        query_block,
                        key_block,
                        (((1,), (1,)), ((), ())),
                        preferred_element_type=jnp.float32,
                    )
                    * scale
                )
                scores = jnp.where(allowed, scores, -jnp.inf)
                top = jnp.max(scores, axis=1, keepdims=True)
                expo = jnp.where(allowed, jnp.exp(scores - top), 0.0)
                probs = expo / jnp.sum(expo, axis=1, keepdims=True)
                probs_b = probs.astype(jnp.bfloat16)
                value_acc = value_acc.at[:last].add(
                    lax.dot_general(
                        probs_b,
                        grad_block,
                        (((0,), (0,)), ((), ())),
                        preferred_element_type=jnp.float32,
                    )
                )
                prob_grad = lax.dot_general(
                    grad_block,
                    value_block,
                    (((1,), (1,)), ((), ())),
                    preferred_element_type=jnp.float32,
                )
                delta = jnp.sum(probs * prob_grad, axis=1, keepdims=True)
                score_grad = (probs * (prob_grad - delta) * scale).astype(jnp.bfloat16)
                query_parts[number][head] = jnp.dot(
                    score_grad, key_block, preferred_element_type=jnp.float32
                ).astype(jnp.bfloat16)
                key_acc = key_acc.at[:last].add(
                    lax.dot_general(
                        score_grad,
                        query_block,
                        (((0,), (0,)), ((), ())),
                        preferred_element_type=jnp.float32,
                    )
                )
        key_groups.append(key_acc)
        value_groups.append(value_acc)
    head_query_grad = jnp.concatenate(
        [jnp.concatenate(parts, axis=1) for parts in query_parts], axis=0
    )
    rows_pos = jnp.arange(length)
    key_total = jnp.stack(key_groups, axis=1)
    key_grad = unrotate(key_total, rows_pos).reshape(length, kv_heads * HD).astype(jnp.bfloat16)
    value_grad = jnp.concatenate(value_groups, axis=1).astype(jnp.bfloat16)
    query_grad = lax.all_to_all(head_query_grad, "seq", split_axis=0, concat_axis=1, tiled=True)
    width = normed.shape[1]
    piece = lax.all_gather(normed, "seq", axis=0, tiled=True)
    key_part = lax.dot_general(
        piece, key_grad, (((0,), (0,)), ((), ())), preferred_element_type=jnp.float32
    )
    value_part = lax.dot_general(
        piece, value_grad, (((0,), (0,)), ((), ())), preferred_element_type=jnp.float32
    )
    key_full, value_full = lax.psum((key_part, value_part), "dp")
    share = width // lax.axis_size("dp")
    offset = lax.axis_index("dp") * share
    key_weight_grad = lax.dynamic_slice_in_dim(key_full, offset, share, 0)
    value_weight_grad = lax.dynamic_slice_in_dim(value_full, offset, share, 0)
    return (query_grad, key_weight_grad, value_weight_grad)


CORE, XBIT, ZLOW, ZHIGH = 1, 2, 4, 8


def flip(array, mask):
    return lax.ppermute(array, "dp", [(i, i ^ mask) for i in range(16)])


def swap_seq(array):
    return lax.ppermute(array, "seq", [(0, 1), (1, 0)])


def params(limit=VMEM_LIMIT):
    return pltpu.CompilerParams(vmem_limit_bytes=limit)


def vmem():
    return pl.BlockSpec(memory_space=pltpu.VMEM)


def smem():
    return pl.BlockSpec(memory_space=pltpu.SMEM)


def rotary_tables(length):
    half = HD // 2
    freqs = np.exp(-math.log(500000.0) * (2.0 * np.arange(half, dtype=np.float64) / HD))
    angle = np.arange(length, dtype=np.float64)[:, None] * freqs[None, :]
    cosine = np.concatenate([np.cos(angle), np.cos(angle)], axis=1)
    sine = np.concatenate([np.sin(angle), -np.sin(angle)], axis=1)
    return cosine.astype(np.float32), sine.astype(np.float32)


def hbm():
    return pl.BlockSpec(memory_space=pltpu.HBM)


def in_hbm(array):
    return pltpu.with_memory_space_constraint(array, pltpu.HBM)


def run_copies(copies):
    for copy in copies:
        copy.start()
    for copy in copies:
        copy.wait()


def prepare(keys, values, normed, me):
    rows, kv_width = keys.shape
    width = normed.shape[1]
    share = width // 16
    wide = kv_width // (2 * NC)


    def body(me_ref, k_hbm, v_hbm, x_hbm, k_ref, v_ref, *rest):
        kv, parts, (x_ref, sem) = rest[:NC], rest[NC : NC + 4], rest[NC + 4 :]
        mine = me_ref[0]
        run_copies(
            [
                pltpu.make_async_copy(k_hbm, k_ref, sem.at[0]),
                pltpu.make_async_copy(v_hbm, v_ref, sem.at[1]),
                pltpu.make_async_copy(x_hbm, x_ref, sem.at[2]),
            ]
        )
        for chunk, out in enumerate(kv):
            for number, ref in enumerate((k_ref, v_ref)):
                for half in range(2):
                    low = (half * NC + chunk) * wide
                    at = (number * 2 + half) * wide
                    out[:, at : at + wide] = ref[:, low : low + wide]

        for place, part in enumerate(parts):
            for number, mask in enumerate((ZHIGH, ZHIGH | CORE, 0, CORE)):
                low = pl.multiple_of((mine ^ (mask | (place * 2))) * share, share)
                part[number] = x_ref[:, pl.ds(low, share)]

    return pl.pallas_call(
        body,
        out_shape=[pltpu.VMEM((rows, kv_width), BF)] * 2
        + [pltpu.VMEM((rows, 4 * wide), BF)] * NC
        + [pltpu.VMEM((4, rows, share), BF)] * 4,
        in_specs=[smem()] + [hbm()] * 3,
        out_specs=[vmem()] * (6 + NC),
        scratch_shapes=[pltpu.VMEM((rows, width), BF), pltpu.SemaphoreType.DMA((3,))],
        compiler_params=params(),
        name="prepare",
    )(me, in_hbm(keys), in_hbm(values), in_hbm(normed))


def stage(arrays):
    count = len(arrays)

    def body(*refs):
        run_copies(
            [
                pltpu.make_async_copy(refs[n], refs[count + n], refs[-1].at[n])
                for n in range(count)
            ]
        )

    return pl.pallas_call(
        body,
        out_shape=[pltpu.VMEM(one.shape, one.dtype) for one in arrays],
        in_specs=[hbm()] * count,
        out_specs=[vmem()] * count,
        scratch_shapes=[pltpu.SemaphoreType.DMA((count,))],
        compiler_params=params(),
        name="stage",
    )(*[in_hbm(one) for one in arrays])


def join_cores(same, recv, after):
    def body(a_ref, b_ref, *refs):
        out = refs[-1]
        for place in range(4):
            out[place, 0] = a_ref[place]
            out[place, 1] = b_ref[place]

    return pl.pallas_call(
        body,
        out_shape=pltpu.VMEM((4, 2) + same.shape[1:], BF),
        in_specs=[vmem()] * 2 + [hbm()] * len(after),
        out_specs=vmem(),
        compiler_params=params(),
        name="join_cores",
    )(same, recv, *after)


def pack_normed(parts, numbers, after):
    rows, share = parts[0].shape[1:]
    shapes = [(4,) + (len(group),) * (len(group) > 1) + (rows, share) for group in numbers]

    def body(*refs):
        for group, out in zip(numbers, refs[-len(numbers) :]):
            for place in range(4):
                if len(group) > 1:
                    for at, number in enumerate(group):
                        out[place, at] = refs[place][number]
                else:
                    out[place] = refs[place][group[0]]

    return pl.pallas_call(
        body,
        out_shape=[pltpu.VMEM(shape, BF) for shape in shapes],
        in_specs=[vmem()] * 4 + [hbm()] * len(after),
        out_specs=[vmem()] * len(shapes),
        compiler_params=params(),
        name="pack_normed",
    )(*parts, *after)


def combine(seq_at, keep_a, keep_b, recv, after):
    rows, wide = keep_a.shape

    def body(at_ref, a_ref, b_ref, recv_ref, *rest):
        out = rest[-1]
        early = (a_ref[...] + recv_ref[:rows].astype(F32)).astype(BF)

        @pl.when(at_ref[0] == 0)
        def _():
            out[:rows] = early
            out[rows:] = recv_ref[rows:]

        @pl.when(at_ref[0] == 1)
        def _():
            out[:rows] = b_ref[...]
            out[rows:] = early

    return pl.pallas_call(
        body,
        out_shape=jax.ShapeDtypeStruct((2 * rows, wide), BF),
        in_specs=[smem(), vmem(), vmem(), vmem()] + [hbm()] * len(after),
        out_specs=vmem(),
        compiler_params=params(),
        name="combine",
    )(seq_at, keep_a, keep_b, recv, *after)


def attention(
    chunk, seq_at, queries, out_grad, keys, values, kv_recv, cosine, sine, after
):
    rows, width = queries.shape
    wide = width // (2 * NC)
    kv_wide = keys.shape[1] // (2 * NC)
    kv_heads = kv_wide // HD
    groups = wide // kv_wide
    span = groups * rows
    scale = 1.0 / math.sqrt(HD)

    def rotate(grad, cos, sin):
        return grad * cos + pltpu.roll(grad, HD // 2, 1) * sin

    def nt(a, b):
        return lax.dot_general(a, b, (((1,), (1,)), ((), ())), preferred_element_type=F32)

    def tn(a, b):
        return lax.dot_general(a, b, (((0,), (0,)), ((), ())), preferred_element_type=F32)

    def body(at_ref, q_ref, g_ref, k_ref, v_ref, kv_ref, cos_ref, sin_ref, *rest):
        qg_ref, keep_a, keep_b, send = rest[-4:]
        late = at_ref[0]

        def columns(j, size):
            return pl.ds(pl.multiple_of(((late ^ j) * NC + chunk) * size, size), size)

        for j in (1, 0):
            one_side(
                j, late,
                q_ref.at[:, columns(j, wide)], g_ref.at[:, columns(j, wide)],
                k_ref.at[:, columns(j, kv_wide)], v_ref.at[:, columns(j, kv_wide)],
                kv_ref, cos_ref, sin_ref, qg_ref.at[j], keep_a, keep_b, send,
            )

    def one_side(
        other, late, q_ref, g_ref, k_ref, v_ref, kv_ref, cos_ref, sin_ref, qg_ref, keep_a, keep_b, send
    ):
        def earlier(number, head):
            low = (number * 2 + (late ^ other)) * kv_wide + head * HD
            return kv_ref[:, pl.ds(pl.multiple_of(low, HD), HD)]

        def stack(ref, head):
            return jnp.concatenate(
                [
                    ref[:, (head * groups + m) * HD : (head * groups + m + 1) * HD]
                    for m in range(groups)
                ],
                axis=0,
            )

        def one_head(head, is_late):
            cols = slice(head * HD, (head + 1) * HD)
            qs = stack(q_ref, head)
            gs = stack(g_ref, head)
            ks = k_ref[:, cols]
            vs = v_ref[:, cols]
            if is_late:
                ks = jnp.concatenate([earlier(0, head), ks], axis=0)
                vs = jnp.concatenate([earlier(1, head), vs], axis=0)
            count = ks.shape[0]
            scores = nt(ks, qs)
            key_pos = lax.broadcasted_iota(jnp.int32, (rows, span), 0)
            query_pos = lax.broadcasted_iota(jnp.int32, (rows, span), 1) % rows
            diagonal = jnp.where(key_pos <= query_pos, scores[count - rows :], -1e30)
            scores = jnp.concatenate([scores[:rows], diagonal], axis=0) if is_late else diagonal
            top = jnp.max(scores, axis=0, keepdims=True)
            expo = jnp.exp2((scores - top) * (scale / math.log(2.0)))
            probs = expo * (1.0 / jnp.sum(expo, axis=0, keepdims=True))
            value_grad = jnp.dot(probs.astype(BF), gs, preferred_element_type=F32)
            prob_grad = nt(vs, gs)
            delta = jnp.sum(probs * prob_grad, axis=0, keepdims=True)
            score_grad = (probs * (prob_grad - delta) * scale).astype(BF)
            key_grad = jnp.dot(score_grad, qs, preferred_element_type=F32)
            query_grad = tn(score_grad, ks).astype(BF)
            for m in range(groups):
                low = (head * groups + m) * HD
                qg_ref[:, low : low + HD] = query_grad[m * rows : (m + 1) * rows]
            first = (rotate(key_grad[:rows], cos_ref[:rows], sin_ref[:rows]), value_grad[:rows])
            second = None
            if is_late:
                second = (
                    rotate(key_grad[rows:], cos_ref[rows:], sin_ref[rows:]),
                    value_grad[rows:],
                )
            return first, second

        def all_heads(is_late):
            parts = [one_head(head, is_late) for head in range(kv_heads)]

            def write(first_ref, second_ref, second_at):
                for head, (first, second) in enumerate(parts):
                    for number in range(2):
                        at = slice(number * kv_wide + head * HD, number * kv_wide + (head + 1) * HD)
                        first_ref[:rows, at] = first[number].astype(first_ref.dtype)
                        later = jnp.zeros((rows, HD), BF) if second is None else second[number].astype(BF)
                        second_ref[second_at : second_at + rows, at] = later

            if other == 0:
                write(keep_a, keep_b, 0)
            else:
                write(send, send, rows)

        @pl.when(late == 1)
        def _():
            all_heads(True)

        @pl.when(late == 0)
        def _():
            all_heads(False)

    operands = [seq_at, queries, out_grad, keys, values, kv_recv, cosine, sine]
    return pl.pallas_call(
        body,
        out_shape=[
            pltpu.VMEM((2, rows, wide), BF),
            pltpu.VMEM((rows, 2 * kv_wide), F32),
            pltpu.VMEM((rows, 2 * kv_wide), BF),
            pltpu.VMEM((2 * rows, 2 * kv_wide), BF),
        ],
        in_specs=[smem()] + [vmem()] * 7 + [hbm()] * len(after),
        out_specs=[vmem()] * 4,
        compiler_params=params(),
        name="attention",
    )(*operands, *after)


def tn(a, b):
    return lax.dot_general(a, b, (((0,), (0,)), ((), ())), preferred_element_type=F32)


def project_away(normed_own, normed_other, grads, after):
    share = normed_own.shape[3]
    wide = grads[0].shape[1]

    def body(xa_ref, xb_ref, *refs):
        ys, keep, sends = refs[:4], refs[-1 - CUT], refs[-CUT:]
        right = jnp.concatenate([ref[...] for ref in ys], axis=0)

        def total(core):
            left = [x_ref[place, core] for place in range(4) for x_ref in (xa_ref, xb_ref)]
            return tn(jnp.concatenate(left, axis=0), right)

        keep[...] = total(0)
        sent = total(1)
        for n, out in enumerate(sends):
            out[...] = sent[n * share // CUT : (n + 1) * share // CUT]

    return pl.pallas_call(
        body,
        out_shape=[pltpu.VMEM((share, wide), F32)] + [pltpu.VMEM((share // CUT, wide), F32)] * CUT,
        in_specs=[vmem()] * 6 + [hbm()] * len(after),
        out_specs=[vmem()] * (1 + CUT),
        compiler_params=params(),
        name="project_away",
    )(normed_own, normed_other, *grads, *after)


def add_round(own, recv, after):
    rows = own.shape[0] // CUT

    def body(a_ref, *refs):
        out = refs[-1]
        for n, b_ref in enumerate(refs[:CUT]):
            at = slice(n * rows, (n + 1) * rows)
            out[at] = (a_ref[at] + b_ref[...]).astype(BF)

    return pl.pallas_call(
        body,
        out_shape=pltpu.VMEM(own.shape, BF),
        in_specs=[vmem()] * (1 + CUT) + [hbm()] * len(after),
        out_specs=vmem(),
        compiler_params=params(),
        name="add_round",
    )(own, *recv, *after)


def join_places(grads, after):
    length, wide = grads[0].shape

    def body(*refs):
        out = refs[-1]
        for place, ref in enumerate(refs[:4]):
            out[place * length : (place + 1) * length] = ref[...]

    return pl.pallas_call(
        body,
        out_shape=pltpu.VMEM((4 * length, wide), BF),
        in_specs=[vmem()] * 4 + [hbm()] * len(after),
        out_specs=vmem(),
        compiler_params=params(),
        name="join_places",
    )(*grads, *after)


def project_home(seq_at, normed, grads, recv, query_grads, after):
    rows, share = normed[0].shape[2:]
    wide = grads[0][0].shape[1]
    chunks = len(grads)
    part = query_grads[0].shape[2]

    def body(at_ref, xa_ref, xb_ref, *refs):
        ys, refs = refs[: 4 * chunks], refs[4 * chunks :]
        others, qs = refs[:chunks], refs[chunks : 2 * chunks]
        out, query_out, sem = refs[-3:]
        copies = []
        for chunk, ref in enumerate(qs):
            for j in range(2):
                low = pl.multiple_of(((at_ref[0] ^ j) * chunks + chunk) * part, part)
                copies.append(
                    pltpu.make_async_copy(ref.at[j], query_out.at[:, pl.ds(low, part)], sem.at[chunk, j])
                )
        for copy in copies:
            copy.start()
        left = [
            x_ref[place, core] for place in range(4) for x_ref in (xa_ref, xb_ref) for core in range(2)
        ]
        left = jnp.concatenate(left, axis=0)
        for chunk in range(chunks):
            right = []
            for place in range(4):
                for seq in range(2):
                    right.append(ys[chunk * 4 + place][seq * rows : (seq + 1) * rows, :])
                    low = (place * 2 + seq) * rows
                    right.append(others[chunk][low : low + rows, :])
            out[:, chunk * wide : (chunk + 1) * wide] = tn(left, jnp.concatenate(right, axis=0))
        for copy in copies:
            copy.wait()

    return pl.pallas_call(
        body,
        out_shape=[
            pltpu.VMEM((share, chunks * wide), F32),
            jax.ShapeDtypeStruct((rows, 2 * chunks * part), BF),
        ],
        in_specs=[smem()] + [vmem()] * (2 + 6 * chunks) + [hbm()] * len(after),
        out_specs=[vmem(), hbm()],
        scratch_shapes=[pltpu.SemaphoreType.DMA((chunks, 2))],
        compiler_params=params(),
        name="project_home",
    )(seq_at, *normed, *[part for parts in grads for part in parts], *recv, *query_grads, *after)


def finish(keep, recv_half):
    rows, width = keep.shape
    wide = width // NC
    part = wide // 2

    def body(keep_ref, *refs):
        halves, outs = refs[:NC], refs[NC:]
        for chunk, half_ref in enumerate(halves):
            for number, out in enumerate(outs):
                low = number * part
                at = slice(chunk * wide + low, chunk * wide + low + part)
                out[:, chunk * part : (chunk + 1) * part] = (
                    keep_ref[:, at] + half_ref[:, low : low + part].astype(F32)
                )

    return pl.pallas_call(
        body,
        out_shape=[jax.ShapeDtypeStruct((rows, width // 2), F32)] * 2,
        in_specs=[vmem()] * (1 + NC),
        out_specs=[vmem()] * 2,
        compiler_params=params(),
        name="finish",
    )(keep, *recv_half)


def cube_local(queries, keys, values, out_grad, normed):
    seq_at = jnp.reshape(lax.axis_index("seq"), (1,)).astype(jnp.int32)
    me = jnp.reshape(lax.axis_index("dp"), (1,)).astype(jnp.int32)
    rows = queries.shape[0]
    cosine, sine = (jnp.asarray(table) for table in rotary_tables(2 * rows))

    keys, values, *rest = prepare(keys, values, normed, me)
    kv, parts = rest[:NC], rest[NC:]
    kv_recv = [lax.ppermute(part, "seq", [(0, 1)]) for part in kv]
    masks = (0, XBIT, ZLOW, XBIT | ZLOW)
    parts = [flip(part, mask) if mask else part for part, mask in zip(parts, masks)]
    q_in, g_in, cosine, sine = stage([queries, out_grad, cosine, sine])

    query_grads, made = [], []
    for chunk in range(NC):
        query_grad, *rest = attention(
            chunk, seq_at, q_in, g_in, keys, values, kv_recv[chunk], cosine, sine,
            parts[1:] + query_grads if chunk else [],
        )
        query_grads.append(query_grad)
        made.append(rest)

    grads = []
    after = [made[-1][0]]
    for keep_a, keep_b, send in made:
        mine = combine(seq_at, keep_a, keep_b, swap_seq(send), after)
        below = flip(mine, ZLOW)
        grads.append([mine, flip(mine, XBIT), below, flip(below, XBIT)])
        after = [grads[-1][1]]

    (away,) = pack_normed(parts, [(0, 1)], [made[-1][0]])
    away_other = swap_seq(away)
    same, cross = pack_normed(parts, [(2,), (3,)], [made[-1][0]])
    cross = flip(cross, CORE)

    recv_half, recv_core = [], []
    after, fence = [grads[1][2], cross], [grads[1][1]]
    for part in grads:
        own, *sends = project_away(away, away_other, part, after)
        total = add_round(own, [flip(send, CORE) for send in sends], fence)
        gathered = join_places(part, [total] + recv_half)
        recv_core.append(flip(gathered, CORE))
        recv_half.append(flip(total, ZHIGH))
        if part is grads[0]:
            home = join_cores(same, cross, [away_other])
            home_other = swap_seq(home)
            after, fence = recv_core[:], [home_other]
    keep, query_grad = project_home(seq_at, (home, home_other), grads, recv_core, query_grads, [total])
    key_weight_grad, value_weight_grad = finish(keep, recv_half)
    return (query_grad, key_weight_grad, value_weight_grad)


def solution(mesh):
    spread = P(("dp", "seq"), None)
    cube = dict(mesh.shape) == {"dp": 16, "seq": 2}
    return jax.shard_map(
        cube_local if cube else general_local,
        mesh=mesh,
        in_specs=(spread,) * 5,
        out_specs=(spread, P("dp", "seq"), P("dp", "seq")),
        check_vma=False,
    )
```

```python
import math

import jax
import jax.numpy as jnp
import numpy as np
from jax import lax
from jax.experimental import pallas as pl
from jax.experimental.pallas import tpu as pltpu
from jax.sharding import PartitionSpec as P

HD = 128
NC = 2
BF = jnp.bfloat16
F32 = jnp.float32
VMEM_LIMIT = 20 * 1024 * 1024
CUT = 4


def unrotate(grad, position):
    half = HD // 2
    freqs = jnp.exp(-math.log(500000.0) * (2.0 * jnp.arange(half).astype(jnp.float32) / HD))
    angle = position.astype(jnp.float32)[:, None] * freqs[None, :]
    cosine = jnp.cos(angle)[:, None, :]
    sine = jnp.sin(angle)[:, None, :]
    first = grad[..., :half]
    second = grad[..., half:]
    return jnp.concatenate(
        [first * cosine + second * sine, second * cosine - first * sine], axis=-1
    )


def general_local(queries, keys, values, out_grad, normed):
    head_q, head_k, head_v, head_g = (
        lax.all_to_all(queries, "seq", split_axis=1, concat_axis=0, tiled=True),
        lax.all_to_all(keys, "seq", split_axis=1, concat_axis=0, tiled=True),
        lax.all_to_all(values, "seq", split_axis=1, concat_axis=0, tiled=True),
        lax.all_to_all(out_grad, "seq", split_axis=1, concat_axis=0, tiled=True),
    )
    length = head_q.shape[0]
    heads = head_q.shape[1] // HD
    kv_heads = head_k.shape[1] // HD
    groups = heads // kv_heads
    scale = 1.0 / math.sqrt(HD)
    block = length if length <= 512 else max(512, length // 8)
    starts = list(range(0, length, block))
    query_parts = [[None] * heads for first in starts]
    key_groups = []
    value_groups = []
    for group in range(kv_heads):
        low = group * HD
        high = low + HD
        key_acc = jnp.zeros((length, HD), jnp.float32)
        value_acc = jnp.zeros((length, HD), jnp.float32)
        for number, first in enumerate(starts):
            last = first + block
            query_pos = first + jnp.arange(block)[:, None]
            key_pos = jnp.arange(last)[None, :]
            allowed = key_pos <= query_pos
            key_block = head_k[:last, low:high]
            value_block = head_v[:last, low:high]
            for member in range(groups):
                head = group * groups + member
                query_block = head_q[first:last, head * HD : (head + 1) * HD]
                grad_block = head_g[first:last, head * HD : (head + 1) * HD]
                scores = (
                    lax.dot_general(
                        query_block,
                        key_block,
                        (((1,), (1,)), ((), ())),
                        preferred_element_type=jnp.float32,
                    )
                    * scale
                )
                scores = jnp.where(allowed, scores, -jnp.inf)
                top = jnp.max(scores, axis=1, keepdims=True)
                expo = jnp.where(allowed, jnp.exp(scores - top), 0.0)
                probs = expo / jnp.sum(expo, axis=1, keepdims=True)
                probs_b = probs.astype(jnp.bfloat16)
                value_acc = value_acc.at[:last].add(
                    lax.dot_general(
                        probs_b,
                        grad_block,
                        (((0,), (0,)), ((), ())),
                        preferred_element_type=jnp.float32,
                    )
                )
                prob_grad = lax.dot_general(
                    grad_block,
                    value_block,
                    (((1,), (1,)), ((), ())),
                    preferred_element_type=jnp.float32,
                )
                delta = jnp.sum(probs * prob_grad, axis=1, keepdims=True)
                score_grad = (probs * (prob_grad - delta) * scale).astype(jnp.bfloat16)
                query_parts[number][head] = jnp.dot(
                    score_grad, key_block, preferred_element_type=jnp.float32
                ).astype(jnp.bfloat16)
                key_acc = key_acc.at[:last].add(
                    lax.dot_general(
                        score_grad,
                        query_block,
                        (((0,), (0,)), ((), ())),
                        preferred_element_type=jnp.float32,
                    )
                )
        key_groups.append(key_acc)
        value_groups.append(value_acc)
    head_query_grad = jnp.concatenate(
        [jnp.concatenate(parts, axis=1) for parts in query_parts], axis=0
    )
    rows_pos = jnp.arange(length)
    key_total = jnp.stack(key_groups, axis=1)
    key_grad = unrotate(key_total, rows_pos).reshape(length, kv_heads * HD).astype(jnp.bfloat16)
    value_grad = jnp.concatenate(value_groups, axis=1).astype(jnp.bfloat16)
    query_grad = lax.all_to_all(head_query_grad, "seq", split_axis=0, concat_axis=1, tiled=True)
    width = normed.shape[1]
    piece = lax.all_gather(normed, "seq", axis=0, tiled=True)
    key_part = lax.dot_general(
        piece, key_grad, (((0,), (0,)), ((), ())), preferred_element_type=jnp.float32
    )
    value_part = lax.dot_general(
        piece, value_grad, (((0,), (0,)), ((), ())), preferred_element_type=jnp.float32
    )
    key_full, value_full = lax.psum((key_part, value_part), "dp")
    share = width // lax.axis_size("dp")
    offset = lax.axis_index("dp") * share
    key_weight_grad = lax.dynamic_slice_in_dim(key_full, offset, share, 0)
    value_weight_grad = lax.dynamic_slice_in_dim(value_full, offset, share, 0)
    return (query_grad, key_weight_grad, value_weight_grad)


CORE, XBIT, ZLOW, ZHIGH = 1, 2, 4, 8


def flip(array, mask):
    return lax.ppermute(array, "dp", [(i, i ^ mask) for i in range(16)])


def swap_seq(array):
    return lax.ppermute(array, "seq", [(0, 1), (1, 0)])


def params(limit=VMEM_LIMIT):
    return pltpu.CompilerParams(vmem_limit_bytes=limit)


def vmem():
    return pl.BlockSpec(memory_space=pltpu.VMEM)


def smem():
    return pl.BlockSpec(memory_space=pltpu.SMEM)


def rotary_tables(length):
    half = HD // 2
    freqs = np.exp(-math.log(500000.0) * (2.0 * np.arange(half, dtype=np.float64) / HD))
    angle = np.arange(length, dtype=np.float64)[:, None] * freqs[None, :]
    cosine = np.concatenate([np.cos(angle), np.cos(angle)], axis=1)
    sine = np.concatenate([np.sin(angle), -np.sin(angle)], axis=1)
    return cosine.astype(np.float32), sine.astype(np.float32)


def hbm():
    return pl.BlockSpec(memory_space=pltpu.HBM)


def in_hbm(array):
    return pltpu.with_memory_space_constraint(array, pltpu.HBM)


def run_copies(copies):
    for copy in copies:
        copy.start()
    for copy in copies:
        copy.wait()


def prepare_kv(keys, values):
    rows, kv_width = keys.shape
    wide = kv_width // (2 * NC)

    def body(k_hbm, v_hbm, k_ref, v_ref, *rest):
        kv, sem = rest[:NC], rest[NC]
        run_copies(
            [
                pltpu.make_async_copy(k_hbm, k_ref, sem.at[0]),
                pltpu.make_async_copy(v_hbm, v_ref, sem.at[1]),
            ]
        )
        for chunk, out in enumerate(kv):
            for number, ref in enumerate((k_ref, v_ref)):
                for half in range(2):
                    low = (half * NC + chunk) * wide
                    at = (number * 2 + half) * wide
                    out[:, at : at + wide] = ref[:, low : low + wide]

    return pl.pallas_call(
        body,
        out_shape=[pltpu.VMEM((rows, kv_width), BF)] * 2 + [pltpu.VMEM((rows, 4 * wide), BF)] * NC,
        in_specs=[hbm()] * 2,
        out_specs=[vmem()] * (2 + NC),
        scratch_shapes=[pltpu.SemaphoreType.DMA((2,))],
        compiler_params=params(),
        name="prepare_kv",
    )(in_hbm(keys), in_hbm(values))


def prepare_normed(normed, me, after):
    rows, width = normed.shape
    share = width // 16

    def body(me_ref, x_hbm, after_ref, *rest):
        parts, (x_ref, sem) = rest[:4], rest[4:]
        mine = me_ref[0]
        run_copies([pltpu.make_async_copy(x_hbm, x_ref, sem)])
        for place, part in enumerate(parts):
            for number, mask in enumerate((ZHIGH, ZHIGH | CORE, 0, CORE)):
                low = pl.multiple_of((mine ^ (mask | (place * 2))) * share, share)
                part[number] = x_ref[:, pl.ds(low, share)]

    return pl.pallas_call(
        body,
        out_shape=[pltpu.VMEM((4, rows, share), BF)] * 4,
        in_specs=[smem(), hbm(), hbm()],
        out_specs=[vmem()] * 4,
        scratch_shapes=[pltpu.VMEM((rows, width), BF), pltpu.SemaphoreType.DMA],
        compiler_params=params(),
        name="prepare_normed",
    )(me, in_hbm(normed), after)


def stage(arrays):
    count = len(arrays)

    def body(*refs):
        run_copies(
            [
                pltpu.make_async_copy(refs[n], refs[count + n], refs[-1].at[n])
                for n in range(count)
            ]
        )

    return pl.pallas_call(
        body,
        out_shape=[pltpu.VMEM(one.shape, one.dtype) for one in arrays],
        in_specs=[hbm()] * count,
        out_specs=[vmem()] * count,
        scratch_shapes=[pltpu.SemaphoreType.DMA((count,))],
        compiler_params=params(),
        name="stage",
    )(*[in_hbm(one) for one in arrays])


def join_cores(same, recv, after):
    def body(a_ref, b_ref, *refs):
        out = refs[-1]
        for place in range(4):
            out[place, 0] = a_ref[place]
            out[place, 1] = b_ref[place]

    return pl.pallas_call(
        body,
        out_shape=pltpu.VMEM((4, 2) + same.shape[1:], BF),
        in_specs=[vmem()] * 2 + [hbm()] * len(after),
        out_specs=vmem(),
        compiler_params=params(),
        name="join_cores",
    )(same, recv, *after)


def pack_normed(parts, numbers, after):
    rows, share = parts[0].shape[1:]
    shapes = [(4,) + (len(group),) * (len(group) > 1) + (rows, share) for group in numbers]

    def body(*refs):
        for group, out in zip(numbers, refs[-len(numbers) :]):
            for place in range(4):
                if len(group) > 1:
                    for at, number in enumerate(group):
                        out[place, at] = refs[place][number]
                else:
                    out[place] = refs[place][group[0]]

    return pl.pallas_call(
        body,
        out_shape=[pltpu.VMEM(shape, BF) for shape in shapes],
        in_specs=[vmem()] * 4 + [hbm()] * len(after),
        out_specs=[vmem()] * len(shapes),
        compiler_params=params(),
        name="pack_normed",
    )(*parts, *after)


def combine(seq_at, keep_a, keep_b, recv, after):
    rows, wide = keep_a.shape

    def body(at_ref, a_ref, b_ref, recv_ref, *rest):
        out = rest[-1]
        early = (a_ref[...] + recv_ref[:rows].astype(F32)).astype(BF)

        @pl.when(at_ref[0] == 0)
        def _():
            out[:rows] = early
            out[rows:] = recv_ref[rows:]

        @pl.when(at_ref[0] == 1)
        def _():
            out[:rows] = b_ref[...]
            out[rows:] = early

    return pl.pallas_call(
        body,
        out_shape=jax.ShapeDtypeStruct((2 * rows, wide), BF),
        in_specs=[smem(), vmem(), vmem(), vmem()] + [hbm()] * len(after),
        out_specs=vmem(),
        compiler_params=params(),
        name="combine",
    )(seq_at, keep_a, keep_b, recv, *after)


def attention(
    chunk, seq_at, queries, out_grad, keys, values, kv_recv, cosine, sine, after
):
    rows, width = queries.shape
    wide = width // (2 * NC)
    kv_wide = keys.shape[1] // (2 * NC)
    kv_heads = kv_wide // HD
    groups = wide // kv_wide
    span = groups * rows
    scale = 1.0 / math.sqrt(HD)

    def rotate(grad, cos, sin):
        return grad * cos + pltpu.roll(grad, HD // 2, 1) * sin

    def nt(a, b):
        return lax.dot_general(a, b, (((1,), (1,)), ((), ())), preferred_element_type=F32)

    def tn(a, b):
        return lax.dot_general(a, b, (((0,), (0,)), ((), ())), preferred_element_type=F32)

    def body(at_ref, q_ref, g_ref, k_ref, v_ref, kv_ref, cos_ref, sin_ref, *rest):
        qg_ref, keep_a, keep_b, send = rest[-4:]
        late = at_ref[0]

        def columns(j, size):
            return pl.ds(pl.multiple_of(((late ^ j) * NC + chunk) * size, size), size)

        for j in (1, 0):
            one_side(
                j, late,
                q_ref.at[:, columns(j, wide)], g_ref.at[:, columns(j, wide)],
                k_ref.at[:, columns(j, kv_wide)], v_ref.at[:, columns(j, kv_wide)],
                kv_ref, cos_ref, sin_ref, qg_ref.at[j], keep_a, keep_b, send,
            )

    def one_side(
        other, late, q_ref, g_ref, k_ref, v_ref, kv_ref, cos_ref, sin_ref, qg_ref, keep_a, keep_b, send
    ):
        def earlier(number, head):
            low = (number * 2 + (late ^ other)) * kv_wide + head * HD
            return kv_ref[:, pl.ds(pl.multiple_of(low, HD), HD)]

        def stack(ref, head):
            return jnp.concatenate(
                [
                    ref[:, (head * groups + m) * HD : (head * groups + m + 1) * HD]
                    for m in range(groups)
                ],
                axis=0,
            )

        def one_head(head, is_late):
            cols = slice(head * HD, (head + 1) * HD)
            qs = stack(q_ref, head)
            gs = stack(g_ref, head)
            ks = k_ref[:, cols]
            vs = v_ref[:, cols]
            if is_late:
                ks = jnp.concatenate([earlier(0, head), ks], axis=0)
                vs = jnp.concatenate([earlier(1, head), vs], axis=0)
            count = ks.shape[0]
            scores = nt(ks, qs)
            key_pos = lax.broadcasted_iota(jnp.int32, (rows, span), 0)
            query_pos = lax.broadcasted_iota(jnp.int32, (rows, span), 1) % rows
            diagonal = jnp.where(key_pos <= query_pos, scores[count - rows :], -1e30)
            scores = jnp.concatenate([scores[:rows], diagonal], axis=0) if is_late else diagonal
            top = jnp.max(scores, axis=0, keepdims=True)
            expo = jnp.exp2((scores - top) * (scale / math.log(2.0)))
            probs = expo * (1.0 / jnp.sum(expo, axis=0, keepdims=True))
            value_grad = jnp.dot(probs.astype(BF), gs, preferred_element_type=F32)
            prob_grad = nt(vs, gs)
            delta = jnp.sum(probs * prob_grad, axis=0, keepdims=True)
            score_grad = (probs * (prob_grad - delta) * scale).astype(BF)
            key_grad = jnp.dot(score_grad, qs, preferred_element_type=F32)
            query_grad = tn(score_grad, ks).astype(BF)
            for m in range(groups):
                low = (head * groups + m) * HD
                qg_ref[:, low : low + HD] = query_grad[m * rows : (m + 1) * rows]
            first = (rotate(key_grad[:rows], cos_ref[:rows], sin_ref[:rows]), value_grad[:rows])
            second = None
            if is_late:
                second = (
                    rotate(key_grad[rows:], cos_ref[rows:], sin_ref[rows:]),
                    value_grad[rows:],
                )
            return first, second

        def all_heads(is_late):
            parts = [one_head(head, is_late) for head in range(kv_heads)]

            def write(first_ref, second_ref, second_at):
                for head, (first, second) in enumerate(parts):
                    for number in range(2):
                        at = slice(number * kv_wide + head * HD, number * kv_wide + (head + 1) * HD)
                        first_ref[:rows, at] = first[number].astype(first_ref.dtype)
                        later = jnp.zeros((rows, HD), BF) if second is None else second[number].astype(BF)
                        second_ref[second_at : second_at + rows, at] = later

            if other == 0:
                write(keep_a, keep_b, 0)
            else:
                write(send, send, rows)

        @pl.when(late == 1)
        def _():
            all_heads(True)

        @pl.when(late == 0)
        def _():
            all_heads(False)

    operands = [seq_at, queries, out_grad, keys, values, kv_recv, cosine, sine]
    return pl.pallas_call(
        body,
        out_shape=[
            pltpu.VMEM((2, rows, wide), BF),
            pltpu.VMEM((rows, 2 * kv_wide), F32),
            pltpu.VMEM((rows, 2 * kv_wide), BF),
            pltpu.VMEM((2 * rows, 2 * kv_wide), BF),
        ],
        in_specs=[smem()] + [vmem()] * 7 + [hbm()] * len(after),
        out_specs=[vmem()] * 4,
        compiler_params=params(),
        name="attention",
    )(*operands, *after)


def tn(a, b):
    return lax.dot_general(a, b, (((0,), (0,)), ((), ())), preferred_element_type=F32)


def project_away(normed_own, normed_other, grads, after):
    share = normed_own.shape[3]
    wide = grads[0].shape[1]

    def body(xa_ref, xb_ref, *refs):
        ys, keep, sends = refs[:4], refs[-1 - CUT], refs[-CUT:]
        right = jnp.concatenate([ref[...] for ref in ys], axis=0)

        def total(core):
            left = [x_ref[place, core] for place in range(4) for x_ref in (xa_ref, xb_ref)]
            return tn(jnp.concatenate(left, axis=0), right)

        keep[...] = total(0)
        sent = total(1)
        for n, out in enumerate(sends):
            out[...] = sent[n * share // CUT : (n + 1) * share // CUT]

    return pl.pallas_call(
        body,
        out_shape=[pltpu.VMEM((share, wide), F32)] + [pltpu.VMEM((share // CUT, wide), F32)] * CUT,
        in_specs=[vmem()] * 6 + [hbm()] * len(after),
        out_specs=[vmem()] * (1 + CUT),
        compiler_params=params(),
        name="project_away",
    )(normed_own, normed_other, *grads, *after)


def add_round(own, recv, after):
    rows = own.shape[0] // CUT

    def body(a_ref, *refs):
        out = refs[-1]
        for n, b_ref in enumerate(refs[:CUT]):
            at = slice(n * rows, (n + 1) * rows)
            out[at] = (a_ref[at] + b_ref[...]).astype(BF)

    return pl.pallas_call(
        body,
        out_shape=pltpu.VMEM(own.shape, BF),
        in_specs=[vmem()] * (1 + CUT) + [hbm()] * len(after),
        out_specs=vmem(),
        compiler_params=params(),
        name="add_round",
    )(own, *recv, *after)


def join_places(grads, after):
    length, wide = grads[0].shape

    def body(*refs):
        out = refs[-1]
        for place, ref in enumerate(refs[:4]):
            out[place * length : (place + 1) * length] = ref[...]

    return pl.pallas_call(
        body,
        out_shape=pltpu.VMEM((4 * length, wide), BF),
        in_specs=[vmem()] * 4 + [hbm()] * len(after),
        out_specs=vmem(),
        compiler_params=params(),
        name="join_places",
    )(*grads, *after)


def project_home(seq_at, normed, grads, recv, query_grads, after):
    rows, share = normed[0].shape[2:]
    wide = grads[0][0].shape[1]
    chunks = len(grads)
    part = query_grads[0].shape[2]

    def body(at_ref, xa_ref, xb_ref, *refs):
        ys, refs = refs[: 4 * chunks], refs[4 * chunks :]
        others, qs = refs[:chunks], refs[chunks : 2 * chunks]
        out, query_out, sem = refs[-3:]
        copies = []
        for chunk, ref in enumerate(qs):
            for j in range(2):
                low = pl.multiple_of(((at_ref[0] ^ j) * chunks + chunk) * part, part)
                copies.append(
                    pltpu.make_async_copy(ref.at[j], query_out.at[:, pl.ds(low, part)], sem.at[chunk, j])
                )
        for copy in copies:
            copy.start()
        left = [
            x_ref[place, core] for place in range(4) for x_ref in (xa_ref, xb_ref) for core in range(2)
        ]
        left = jnp.concatenate(left, axis=0)
        for chunk in range(chunks):
            right = []
            for place in range(4):
                for seq in range(2):
                    right.append(ys[chunk * 4 + place][seq * rows : (seq + 1) * rows, :])
                    low = (place * 2 + seq) * rows
                    right.append(others[chunk][low : low + rows, :])
            out[:, chunk * wide : (chunk + 1) * wide] = tn(left, jnp.concatenate(right, axis=0))
        for copy in copies:
            copy.wait()

    return pl.pallas_call(
        body,
        out_shape=[
            pltpu.VMEM((share, chunks * wide), F32),
            jax.ShapeDtypeStruct((rows, 2 * chunks * part), BF),
        ],
        in_specs=[smem()] + [vmem()] * (2 + 6 * chunks) + [hbm()] * len(after),
        out_specs=[vmem(), hbm()],
        scratch_shapes=[pltpu.SemaphoreType.DMA((chunks, 2))],
        compiler_params=params(),
        name="project_home",
    )(seq_at, *normed, *[part for parts in grads for part in parts], *recv, *query_grads, *after)


def finish(keep, recv_half):
    rows, width = keep.shape
    wide = width // NC
    part = wide // 2

    def body(keep_ref, *refs):
        halves, outs = refs[:NC], refs[NC:]
        for chunk, half_ref in enumerate(halves):
            for number, out in enumerate(outs):
                low = number * part
                at = slice(chunk * wide + low, chunk * wide + low + part)
                out[:, chunk * part : (chunk + 1) * part] = (
                    keep_ref[:, at] + half_ref[:, low : low + part].astype(F32)
                )

    return pl.pallas_call(
        body,
        out_shape=[jax.ShapeDtypeStruct((rows, width // 2), F32)] * 2,
        in_specs=[vmem()] * (1 + NC),
        out_specs=[vmem()] * 2,
        compiler_params=params(),
        name="finish",
    )(keep, *recv_half)


def cube_local(queries, keys, values, out_grad, normed):
    seq_at = jnp.reshape(lax.axis_index("seq"), (1,)).astype(jnp.int32)
    me = jnp.reshape(lax.axis_index("dp"), (1,)).astype(jnp.int32)
    rows = queries.shape[0]
    cosine, sine = (jnp.asarray(table) for table in rotary_tables(2 * rows))

    keys, values, *kv = prepare_kv(keys, values)
    parts = prepare_normed(normed, me, kv[0])
    kv_recv = [lax.ppermute(part, "seq", [(0, 1)]) for part in kv]
    masks = (0, XBIT, ZLOW, XBIT | ZLOW)
    parts = [flip(part, mask) if mask else part for part, mask in zip(parts, masks)]
    q_in, g_in, cosine, sine = stage([queries, out_grad, cosine, sine])

    query_grads, made = [], []
    for chunk in range(NC):
        query_grad, *rest = attention(
            chunk, seq_at, q_in, g_in, keys, values, kv_recv[chunk], cosine, sine,
            [parts[1], parts[3]] + query_grads if chunk else [],
        )
        query_grads.append(query_grad)
        made.append(rest)

    grads = []
    after = [made[-1][0]]
    for keep_a, keep_b, send in made:
        mine = combine(seq_at, keep_a, keep_b, swap_seq(send), after)
        below = flip(mine, ZLOW)
        grads.append([mine, flip(mine, XBIT), below, flip(below, XBIT)])
        after = grads[-1][1:3]

    (away,) = pack_normed(parts, [(0, 1)], [made[-1][0]])
    away_other = swap_seq(away)
    same, cross = pack_normed(parts, [(2,), (3,)], [made[-1][0]])
    cross = flip(cross, CORE)

    recv_half, recv_core = [], []
    after, fence = [grads[1][2], cross], [grads[1][1]]
    for part in grads:
        own, *sends = project_away(away, away_other, part, after)
        total = add_round(own, [flip(send, CORE) for send in sends], fence)
        gathered = join_places(part, [total] + recv_half)
        recv_core.append(flip(gathered, CORE))
        recv_half.append(flip(total, ZHIGH))
        if part is grads[0]:
            home = join_cores(same, cross, [away_other])
            home_other = swap_seq(home)
            after, fence = recv_core[:], [home_other]
    keep, query_grad = project_home(seq_at, (home, home_other), grads, recv_core, query_grads, [total])
    key_weight_grad, value_weight_grad = finish(keep, recv_half)
    return (query_grad, key_weight_grad, value_weight_grad)


def solution(mesh):
    spread = P(("dp", "seq"), None)
    cube = dict(mesh.shape) == {"dp": 16, "seq": 2}
    return jax.shard_map(
        cube_local if cube else general_local,
        mesh=mesh,
        in_specs=(spread,) * 5,
        out_specs=(spread, P("dp", "seq"), P("dp", "seq")),
        check_vma=False,
    )
```

```python
import math

import jax
import jax.numpy as jnp
import numpy as np
from jax import lax
from jax.experimental import pallas as pl
from jax.experimental.pallas import tpu as pltpu
from jax.sharding import PartitionSpec as P

HD = 128
NC = 2
BF = jnp.bfloat16
F32 = jnp.float32
VMEM_LIMIT = 20 * 1024 * 1024
CUT = 4


def unrotate(grad, position):
    half = HD // 2
    freqs = jnp.exp(-math.log(500000.0) * (2.0 * jnp.arange(half).astype(jnp.float32) / HD))
    angle = position.astype(jnp.float32)[:, None] * freqs[None, :]
    cosine = jnp.cos(angle)[:, None, :]
    sine = jnp.sin(angle)[:, None, :]
    first = grad[..., :half]
    second = grad[..., half:]
    return jnp.concatenate(
        [first * cosine + second * sine, second * cosine - first * sine], axis=-1
    )


def general_local(queries, keys, values, out_grad, normed):
    head_q, head_k, head_v, head_g = (
        lax.all_to_all(queries, "seq", split_axis=1, concat_axis=0, tiled=True),
        lax.all_to_all(keys, "seq", split_axis=1, concat_axis=0, tiled=True),
        lax.all_to_all(values, "seq", split_axis=1, concat_axis=0, tiled=True),
        lax.all_to_all(out_grad, "seq", split_axis=1, concat_axis=0, tiled=True),
    )
    length = head_q.shape[0]
    heads = head_q.shape[1] // HD
    kv_heads = head_k.shape[1] // HD
    groups = heads // kv_heads
    scale = 1.0 / math.sqrt(HD)
    block = length if length <= 512 else max(512, length // 8)
    starts = list(range(0, length, block))
    query_parts = [[None] * heads for first in starts]
    key_groups = []
    value_groups = []
    for group in range(kv_heads):
        low = group * HD
        high = low + HD
        key_acc = jnp.zeros((length, HD), jnp.float32)
        value_acc = jnp.zeros((length, HD), jnp.float32)
        for number, first in enumerate(starts):
            last = first + block
            query_pos = first + jnp.arange(block)[:, None]
            key_pos = jnp.arange(last)[None, :]
            allowed = key_pos <= query_pos
            key_block = head_k[:last, low:high]
            value_block = head_v[:last, low:high]
            for member in range(groups):
                head = group * groups + member
                query_block = head_q[first:last, head * HD : (head + 1) * HD]
                grad_block = head_g[first:last, head * HD : (head + 1) * HD]
                scores = (
                    lax.dot_general(
                        query_block,
                        key_block,
                        (((1,), (1,)), ((), ())),
                        preferred_element_type=jnp.float32,
                    )
                    * scale
                )
                scores = jnp.where(allowed, scores, -jnp.inf)
                top = jnp.max(scores, axis=1, keepdims=True)
                expo = jnp.where(allowed, jnp.exp(scores - top), 0.0)
                probs = expo / jnp.sum(expo, axis=1, keepdims=True)
                probs_b = probs.astype(jnp.bfloat16)
                value_acc = value_acc.at[:last].add(
                    lax.dot_general(
                        probs_b,
                        grad_block,
                        (((0,), (0,)), ((), ())),
                        preferred_element_type=jnp.float32,
                    )
                )
                prob_grad = lax.dot_general(
                    grad_block,
                    value_block,
                    (((1,), (1,)), ((), ())),
                    preferred_element_type=jnp.float32,
                )
                delta = jnp.sum(probs * prob_grad, axis=1, keepdims=True)
                score_grad = (probs * (prob_grad - delta) * scale).astype(jnp.bfloat16)
                query_parts[number][head] = jnp.dot(
                    score_grad, key_block, preferred_element_type=jnp.float32
                ).astype(jnp.bfloat16)
                key_acc = key_acc.at[:last].add(
                    lax.dot_general(
                        score_grad,
                        query_block,
                        (((0,), (0,)), ((), ())),
                        preferred_element_type=jnp.float32,
                    )
                )
        key_groups.append(key_acc)
        value_groups.append(value_acc)
    head_query_grad = jnp.concatenate(
        [jnp.concatenate(parts, axis=1) for parts in query_parts], axis=0
    )
    rows_pos = jnp.arange(length)
    key_total = jnp.stack(key_groups, axis=1)
    key_grad = unrotate(key_total, rows_pos).reshape(length, kv_heads * HD).astype(jnp.bfloat16)
    value_grad = jnp.concatenate(value_groups, axis=1).astype(jnp.bfloat16)
    query_grad = lax.all_to_all(head_query_grad, "seq", split_axis=0, concat_axis=1, tiled=True)
    width = normed.shape[1]
    piece = lax.all_gather(normed, "seq", axis=0, tiled=True)
    key_part = lax.dot_general(
        piece, key_grad, (((0,), (0,)), ((), ())), preferred_element_type=jnp.float32
    )
    value_part = lax.dot_general(
        piece, value_grad, (((0,), (0,)), ((), ())), preferred_element_type=jnp.float32
    )
    key_full, value_full = lax.psum((key_part, value_part), "dp")
    share = width // lax.axis_size("dp")
    offset = lax.axis_index("dp") * share
    key_weight_grad = lax.dynamic_slice_in_dim(key_full, offset, share, 0)
    value_weight_grad = lax.dynamic_slice_in_dim(value_full, offset, share, 0)
    return (query_grad, key_weight_grad, value_weight_grad)


CORE, XBIT, ZLOW, ZHIGH = 1, 2, 4, 8


def flip(array, mask):
    return lax.ppermute(array, "dp", [(i, i ^ mask) for i in range(16)])


def swap_seq(array):
    return lax.ppermute(array, "seq", [(0, 1), (1, 0)])


def params(limit=VMEM_LIMIT):
    return pltpu.CompilerParams(vmem_limit_bytes=limit)


def vmem():
    return pl.BlockSpec(memory_space=pltpu.VMEM)


def smem():
    return pl.BlockSpec(memory_space=pltpu.SMEM)


def rotary_tables(length):
    half = HD // 2
    freqs = np.exp(-math.log(500000.0) * (2.0 * np.arange(half, dtype=np.float64) / HD))
    angle = np.arange(length, dtype=np.float64)[:, None] * freqs[None, :]
    cosine = np.concatenate([np.cos(angle), np.cos(angle)], axis=1)
    sine = np.concatenate([np.sin(angle), -np.sin(angle)], axis=1)
    return cosine.astype(np.float32), sine.astype(np.float32)


def hbm():
    return pl.BlockSpec(memory_space=pltpu.HBM)


def in_hbm(array):
    return pltpu.with_memory_space_constraint(array, pltpu.HBM)


def run_copies(copies):
    for copy in copies:
        copy.start()
    for copy in copies:
        copy.wait()


def prepare_kv(keys, values):
    rows, kv_width = keys.shape
    wide = kv_width // (2 * NC)

    def body(k_hbm, v_hbm, k_ref, v_ref, *rest):
        kv, sem = rest[:NC], rest[NC]
        run_copies(
            [
                pltpu.make_async_copy(k_hbm, k_ref, sem.at[0]),
                pltpu.make_async_copy(v_hbm, v_ref, sem.at[1]),
            ]
        )
        for chunk, out in enumerate(kv):
            for number, ref in enumerate((k_ref, v_ref)):
                for half in range(2):
                    low = (half * NC + chunk) * wide
                    at = (number * 2 + half) * wide
                    out[:, at : at + wide] = ref[:, low : low + wide]

    return pl.pallas_call(
        body,
        out_shape=[pltpu.VMEM((rows, kv_width), BF)] * 2 + [pltpu.VMEM((rows, 4 * wide), BF)] * NC,
        in_specs=[hbm()] * 2,
        out_specs=[vmem()] * (2 + NC),
        scratch_shapes=[pltpu.SemaphoreType.DMA((2,))],
        compiler_params=params(),
        name="prepare_kv",
    )(in_hbm(keys), in_hbm(values))


def prepare_normed(normed, me, after):
    rows, width = normed.shape
    share = width // 16

    def body(me_ref, x_hbm, after_ref, *rest):
        parts, (x_ref, sem) = rest[:4], rest[4:]
        mine = me_ref[0]
        run_copies([pltpu.make_async_copy(x_hbm, x_ref, sem)])
        for place, part in enumerate(parts):
            for number, mask in enumerate((ZHIGH, ZHIGH | CORE, 0, CORE)):
                low = pl.multiple_of((mine ^ (mask | (place * 2))) * share, share)
                part[number] = x_ref[:, pl.ds(low, share)]

    return pl.pallas_call(
        body,
        out_shape=[pltpu.VMEM((4, rows, share), BF)] * 4,
        in_specs=[smem(), hbm(), hbm()],
        out_specs=[vmem()] * 4,
        scratch_shapes=[pltpu.VMEM((rows, width), BF), pltpu.SemaphoreType.DMA],
        compiler_params=params(),
        name="prepare_normed",
    )(me, in_hbm(normed), after)


def stage(arrays):
    count = len(arrays)

    def body(*refs):
        run_copies(
            [
                pltpu.make_async_copy(refs[n], refs[count + n], refs[-1].at[n])
                for n in range(count)
            ]
        )

    return pl.pallas_call(
        body,
        out_shape=[pltpu.VMEM(one.shape, one.dtype) for one in arrays],
        in_specs=[hbm()] * count,
        out_specs=[vmem()] * count,
        scratch_shapes=[pltpu.SemaphoreType.DMA((count,))],
        compiler_params=params(),
        name="stage",
    )(*[in_hbm(one) for one in arrays])


def join_cores(same, recv, after):
    def body(a_ref, b_ref, *refs):
        out = refs[-1]
        for place in range(4):
            out[place, 0] = a_ref[place]
            out[place, 1] = b_ref[place]

    return pl.pallas_call(
        body,
        out_shape=pltpu.VMEM((4, 2) + same.shape[1:], BF),
        in_specs=[vmem()] * 2 + [hbm()] * len(after),
        out_specs=vmem(),
        compiler_params=params(),
        name="join_cores",
    )(same, recv, *after)


def pack_normed(parts, numbers, after):
    rows, share = parts[0].shape[1:]
    shapes = [(4,) + (len(group),) * (len(group) > 1) + (rows, share) for group in numbers]

    def body(*refs):
        for group, out in zip(numbers, refs[-len(numbers) :]):
            for place in range(4):
                if len(group) > 1:
                    for at, number in enumerate(group):
                        out[place, at] = refs[place][number]
                else:
                    out[place] = refs[place][group[0]]

    return pl.pallas_call(
        body,
        out_shape=[pltpu.VMEM(shape, BF) for shape in shapes],
        in_specs=[vmem()] * 4 + [hbm()] * len(after),
        out_specs=[vmem()] * len(shapes),
        compiler_params=params(),
        name="pack_normed",
    )(*parts, *after)


def combine(seq_at, keep_a, keep_b, recv, after):
    rows, wide = keep_a.shape

    def body(at_ref, a_ref, b_ref, recv_ref, *rest):
        out = rest[-1]
        early = (a_ref[...] + recv_ref[:rows].astype(F32)).astype(BF)

        @pl.when(at_ref[0] == 0)
        def _():
            out[:rows] = early
            out[rows:] = recv_ref[rows:]

        @pl.when(at_ref[0] == 1)
        def _():
            out[:rows] = b_ref[...]
            out[rows:] = early

    return pl.pallas_call(
        body,
        out_shape=jax.ShapeDtypeStruct((2 * rows, wide), BF),
        in_specs=[smem(), vmem(), vmem(), vmem()] + [hbm()] * len(after),
        out_specs=vmem(),
        compiler_params=params(),
        name="combine",
    )(seq_at, keep_a, keep_b, recv, *after)


def attention(
    chunk, seq_at, queries, out_grad, keys, values, kv_recv, cosine, sine, after
):
    rows, width = queries.shape
    wide = width // (2 * NC)
    kv_wide = keys.shape[1] // (2 * NC)
    kv_heads = kv_wide // HD
    groups = wide // kv_wide
    span = groups * rows
    scale = 1.0 / math.sqrt(HD)

    def rotate(grad, cos, sin):
        return grad * cos + pltpu.roll(grad, HD // 2, 1) * sin

    def nt(a, b):
        return lax.dot_general(a, b, (((1,), (1,)), ((), ())), preferred_element_type=F32)

    def tn(a, b):
        return lax.dot_general(a, b, (((0,), (0,)), ((), ())), preferred_element_type=F32)

    def body(at_ref, q_ref, g_ref, k_ref, v_ref, kv_ref, cos_ref, sin_ref, *rest):
        qg_ref, keep_a, keep_b, send = rest[-4:]
        late = at_ref[0]

        def columns(j, size):
            return pl.ds(pl.multiple_of(((late ^ j) * NC + chunk) * size, size), size)

        for j in (1, 0):
            one_side(
                j, late,
                q_ref.at[:, columns(j, wide)], g_ref.at[:, columns(j, wide)],
                k_ref.at[:, columns(j, kv_wide)], v_ref.at[:, columns(j, kv_wide)],
                kv_ref, cos_ref, sin_ref, qg_ref.at[j], keep_a, keep_b, send,
            )

    def one_side(
        other, late, q_ref, g_ref, k_ref, v_ref, kv_ref, cos_ref, sin_ref, qg_ref, keep_a, keep_b, send
    ):
        def earlier(number, head):
            low = (number * 2 + (late ^ other)) * kv_wide + head * HD
            return kv_ref[:, pl.ds(pl.multiple_of(low, HD), HD)]

        def stack(ref, head):
            return jnp.concatenate(
                [
                    ref[:, (head * groups + m) * HD : (head * groups + m + 1) * HD]
                    for m in range(groups)
                ],
                axis=0,
            )

        def one_head(head, is_late):
            cols = slice(head * HD, (head + 1) * HD)
            qs = stack(q_ref, head)
            gs = stack(g_ref, head)
            ks = k_ref[:, cols]
            vs = v_ref[:, cols]
            if is_late:
                ks = jnp.concatenate([earlier(0, head), ks], axis=0)
                vs = jnp.concatenate([earlier(1, head), vs], axis=0)
            count = ks.shape[0]
            scores = nt(ks, qs)
            key_pos = lax.broadcasted_iota(jnp.int32, (rows, span), 0)
            query_pos = lax.broadcasted_iota(jnp.int32, (rows, span), 1) % rows
            diagonal = jnp.where(key_pos <= query_pos, scores[count - rows :], -1e30)
            scores = jnp.concatenate([scores[:rows], diagonal], axis=0) if is_late else diagonal
            top = jnp.max(scores, axis=0, keepdims=True)
            expo = jnp.exp2((scores - top) * (scale / math.log(2.0)))
            probs = expo * (1.0 / jnp.sum(expo, axis=0, keepdims=True))
            value_grad = jnp.dot(probs.astype(BF), gs, preferred_element_type=F32)
            prob_grad = nt(vs, gs)
            delta = jnp.sum(probs * prob_grad, axis=0, keepdims=True)
            score_grad = (probs * (prob_grad - delta) * scale).astype(BF)
            key_grad = jnp.dot(score_grad, qs, preferred_element_type=F32)
            query_grad = tn(score_grad, ks).astype(BF)
            for m in range(groups):
                low = (head * groups + m) * HD
                qg_ref[:, low : low + HD] = query_grad[m * rows : (m + 1) * rows]
            first = (rotate(key_grad[:rows], cos_ref[:rows], sin_ref[:rows]), value_grad[:rows])
            second = None
            if is_late:
                second = (
                    rotate(key_grad[rows:], cos_ref[rows:], sin_ref[rows:]),
                    value_grad[rows:],
                )
            return first, second

        def all_heads(is_late):
            parts = [one_head(head, is_late) for head in range(kv_heads)]

            def write(first_ref, second_ref, second_at):
                for head, (first, second) in enumerate(parts):
                    for number in range(2):
                        at = slice(number * kv_wide + head * HD, number * kv_wide + (head + 1) * HD)
                        first_ref[:rows, at] = first[number].astype(first_ref.dtype)
                        later = jnp.zeros((rows, HD), BF) if second is None else second[number].astype(BF)
                        second_ref[second_at : second_at + rows, at] = later

            if other == 0:
                write(keep_a, keep_b, 0)
            else:
                write(send, send, rows)

        @pl.when(late == 1)
        def _():
            all_heads(True)

        @pl.when(late == 0)
        def _():
            all_heads(False)

    operands = [seq_at, queries, out_grad, keys, values, kv_recv, cosine, sine]
    return pl.pallas_call(
        body,
        out_shape=[
            pltpu.VMEM((2, rows, wide), BF),
            pltpu.VMEM((rows, 2 * kv_wide), F32),
            pltpu.VMEM((rows, 2 * kv_wide), BF),
            pltpu.VMEM((2 * rows, 2 * kv_wide), BF),
        ],
        in_specs=[smem()] + [vmem()] * 7 + [hbm()] * len(after),
        out_specs=[vmem()] * 4,
        compiler_params=params(),
        name="attention",
    )(*operands, *after)


def tn(a, b):
    return lax.dot_general(a, b, (((0,), (0,)), ((), ())), preferred_element_type=F32)


def project_away(normed_own, normed_other, grads, after):
    share = normed_own.shape[3]
    wide = grads[0].shape[1]

    def body(xa_ref, xb_ref, *refs):
        ys, keep, sends = refs[:4], refs[-1 - CUT], refs[-CUT:]
        right = jnp.concatenate([ref[...] for ref in ys], axis=0)

        def total(core):
            left = [x_ref[place, core] for place in range(4) for x_ref in (xa_ref, xb_ref)]
            return tn(jnp.concatenate(left, axis=0), right)

        keep[...] = total(0)
        sent = total(1)
        for n, out in enumerate(sends):
            out[...] = sent[n * share // CUT : (n + 1) * share // CUT]

    return pl.pallas_call(
        body,
        out_shape=[pltpu.VMEM((share, wide), F32)] + [pltpu.VMEM((share // CUT, wide), F32)] * CUT,
        in_specs=[vmem()] * 6 + [hbm()] * len(after),
        out_specs=[vmem()] * (1 + CUT),
        compiler_params=params(),
        name="project_away",
    )(normed_own, normed_other, *grads, *after)


def add_round(own, recv, after):
    rows = own.shape[0] // CUT

    def body(a_ref, *refs):
        out = refs[-1]
        for n, b_ref in enumerate(refs[:CUT]):
            at = slice(n * rows, (n + 1) * rows)
            out[at] = (a_ref[at] + b_ref[...]).astype(BF)

    return pl.pallas_call(
        body,
        out_shape=pltpu.VMEM(own.shape, BF),
        in_specs=[vmem()] * (1 + CUT) + [hbm()] * len(after),
        out_specs=vmem(),
        compiler_params=params(),
        name="add_round",
    )(own, *recv, *after)


def join_places(grads, after):
    length, wide = grads[0].shape

    def body(*refs):
        out = refs[-1]
        for place, ref in enumerate(refs[:4]):
            out[place * length : (place + 1) * length] = ref[...]

    return pl.pallas_call(
        body,
        out_shape=pltpu.VMEM((4 * length, wide), BF),
        in_specs=[vmem()] * 4 + [hbm()] * len(after),
        out_specs=vmem(),
        compiler_params=params(),
        name="join_places",
    )(*grads, *after)


def project_home(seq_at, normed, grads, recv, query_grads, halves, after):
    rows, share = normed[0].shape[2:]
    wide = grads[0][0].shape[1]
    chunks = len(grads)
    part = query_grads[0].shape[2]
    ready = len(halves)
    cols = wide // 2

    def body(at_ref, xa_ref, xb_ref, *refs):
        ys, refs = refs[: 4 * chunks], refs[4 * chunks :]
        others, qs, half_refs = refs[:chunks], refs[chunks : 2 * chunks], refs[2 * chunks : 2 * chunks + ready]
        out, query_out, *outs, sums, sem, sum_sem = refs[-7:]
        copies = []
        for chunk, ref in enumerate(qs):
            for j in range(2):
                low = pl.multiple_of(((at_ref[0] ^ j) * chunks + chunk) * part, part)
                copies.append(
                    pltpu.make_async_copy(ref.at[j], query_out.at[:, pl.ds(low, part)], sem.at[chunk, j])
                )
        for copy in copies:
            copy.start()
        left = [
            x_ref[place, core] for place in range(4) for x_ref in (xa_ref, xb_ref) for core in range(2)
        ]
        left = jnp.concatenate(left, axis=0)
        for chunk in range(chunks):
            right = []
            for place in range(4):
                for seq in range(2):
                    right.append(ys[chunk * 4 + place][seq * rows : (seq + 1) * rows, :])
                    low = (place * 2 + seq) * rows
                    right.append(others[chunk][low : low + rows, :])
            total = tn(left, jnp.concatenate(right, axis=0))
            if chunk >= ready:
                out[:, (chunk - ready) * wide : (chunk - ready + 1) * wide] = total
                continue
            for number in range(2):
                at = slice(number * cols, (number + 1) * cols)
                sums[chunk, number] = total[:, at] + half_refs[chunk][:, at].astype(F32)
                copy = pltpu.make_async_copy(
                    sums.at[chunk, number],
                    outs[number].at[:, chunk * cols : (chunk + 1) * cols],
                    sum_sem.at[chunk, number],
                )
                copy.start()
                copies.append(copy)
        for copy in copies:
            copy.wait()

    return pl.pallas_call(
        body,
        out_shape=[
            pltpu.VMEM((share, (chunks - ready) * wide), F32),
            jax.ShapeDtypeStruct((rows, 2 * chunks * part), BF),
            pltpu.HBM((share, chunks * cols), F32),
            pltpu.HBM((share, chunks * cols), F32),
        ],
        in_specs=[smem()] + [vmem()] * (2 + 6 * chunks + ready) + [hbm()] * len(after),
        out_specs=[vmem(), hbm(), hbm(), hbm()],
        scratch_shapes=[
            pltpu.VMEM((ready, 2, share, cols), F32),
            pltpu.SemaphoreType.DMA((chunks, 2)),
            pltpu.SemaphoreType.DMA((ready, 2)),
        ],
        compiler_params=params(),
        name="project_home",
    )(seq_at, *normed, *[part for parts in grads for part in parts], *recv, *query_grads, *halves, *after)


def finish(keep, recv_half, sums):
    rows, wide = keep.shape
    cols = wide // 2
    low = sums[0].shape[1] - cols

    def body(keep_ref, half_ref, *refs):
        outs, total, sem = refs[2:4], refs[4], refs[5]
        copies = []
        for number, out in enumerate(outs):
            at = slice(number * cols, (number + 1) * cols)
            total[number] = keep_ref[:, at] + half_ref[:, at].astype(F32)
            copies.append(
                pltpu.make_async_copy(total.at[number], out.at[:, low : low + cols], sem.at[number])
            )
            copies[-1].start()
        for copy in copies:
            copy.wait()

    return pl.pallas_call(
        body,
        out_shape=[pltpu.HBM(one.shape, F32) for one in sums],
        in_specs=[vmem()] * 2 + [hbm()] * 2,
        out_specs=[hbm()] * 2,
        scratch_shapes=[pltpu.VMEM((2, rows, cols), F32), pltpu.SemaphoreType.DMA((2,))],
        input_output_aliases={2: 0, 3: 1},
        compiler_params=params(),
        name="finish",
    )(keep, recv_half, *[in_hbm(one) for one in sums])


def cube_local(queries, keys, values, out_grad, normed):
    seq_at = jnp.reshape(lax.axis_index("seq"), (1,)).astype(jnp.int32)
    me = jnp.reshape(lax.axis_index("dp"), (1,)).astype(jnp.int32)
    rows = queries.shape[0]
    cosine, sine = (jnp.asarray(table) for table in rotary_tables(2 * rows))

    keys, values, *kv = prepare_kv(keys, values)
    parts = prepare_normed(normed, me, kv[0])
    kv_recv = [lax.ppermute(part, "seq", [(0, 1)]) for part in kv]
    masks = (0, XBIT, ZLOW, XBIT | ZLOW)
    parts = [flip(part, mask) if mask else part for part, mask in zip(parts, masks)]
    q_in, g_in, cosine, sine = stage([queries, out_grad, cosine, sine])

    query_grads, made = [], []
    for chunk in range(NC):
        query_grad, *rest = attention(
            chunk, seq_at, q_in, g_in, keys, values, kv_recv[chunk], cosine, sine,
            [parts[1], parts[3]] + query_grads if chunk else [],
        )
        query_grads.append(query_grad)
        made.append(rest)

    grads = []
    after = [made[-1][0]]
    for keep_a, keep_b, send in made:
        mine = combine(seq_at, keep_a, keep_b, swap_seq(send), after)
        below = flip(mine, ZLOW)
        grads.append([mine, flip(mine, XBIT), below, flip(below, XBIT)])
        after = grads[-1][1:3]

    (away,) = pack_normed(parts, [(0, 1)], [made[-1][0]])
    away_other = swap_seq(away)
    same, cross = pack_normed(parts, [(2,), (3,)], [made[-1][0]])
    cross = flip(cross, CORE)

    recv_half, recv_core = [], []
    after, fence = [grads[1][2], cross], [grads[1][1]]
    for part in grads:
        own, *sends = project_away(away, away_other, part, after)
        total = add_round(own, [flip(send, CORE) for send in sends], fence)
        gathered = join_places(part, [total] + recv_half)
        recv_core.append(flip(gathered, CORE))
        recv_half.append(flip(total, ZHIGH))
        if part is grads[0]:
            home = join_cores(same, cross, [away_other])
            home_other = swap_seq(home)
            after, fence = recv_core[:], [home_other]
    keep, query_grad, *sums = project_home(
        seq_at, (home, home_other), grads, recv_core, query_grads, recv_half[:-1], [total]
    )
    key_weight_grad, value_weight_grad = finish(keep, recv_half[-1], sums)
    return (query_grad, key_weight_grad, value_weight_grad)


def solution(mesh):
    spread = P(("dp", "seq"), None)
    cube = dict(mesh.shape) == {"dp": 16, "seq": 2}
    return jax.shard_map(
        cube_local if cube else general_local,
        mesh=mesh,
        in_specs=(spread,) * 5,
        out_specs=(spread, P("dp", "seq"), P("dp", "seq")),
        check_vma=False,
    )
```

```python
import math

import jax
import jax.numpy as jnp
import numpy as np
from jax import lax
from jax.experimental import pallas as pl
from jax.experimental.pallas import tpu as pltpu
from jax.sharding import PartitionSpec as P

HD = 128
NC = 2
BF = jnp.bfloat16
F32 = jnp.float32
VMEM_LIMIT = 20 * 1024 * 1024
CUT = 4


def unrotate(grad, position):
    half = HD // 2
    freqs = jnp.exp(-math.log(500000.0) * (2.0 * jnp.arange(half).astype(jnp.float32) / HD))
    angle = position.astype(jnp.float32)[:, None] * freqs[None, :]
    cosine = jnp.cos(angle)[:, None, :]
    sine = jnp.sin(angle)[:, None, :]
    first = grad[..., :half]
    second = grad[..., half:]
    return jnp.concatenate(
        [first * cosine + second * sine, second * cosine - first * sine], axis=-1
    )


def general_local(queries, keys, values, out_grad, normed):
    head_q, head_k, head_v, head_g = (
        lax.all_to_all(queries, "seq", split_axis=1, concat_axis=0, tiled=True),
        lax.all_to_all(keys, "seq", split_axis=1, concat_axis=0, tiled=True),
        lax.all_to_all(values, "seq", split_axis=1, concat_axis=0, tiled=True),
        lax.all_to_all(out_grad, "seq", split_axis=1, concat_axis=0, tiled=True),
    )
    length = head_q.shape[0]
    heads = head_q.shape[1] // HD
    kv_heads = head_k.shape[1] // HD
    groups = heads // kv_heads
    scale = 1.0 / math.sqrt(HD)
    block = length if length <= 512 else max(512, length // 8)
    starts = list(range(0, length, block))
    query_parts = [[None] * heads for first in starts]
    key_groups = []
    value_groups = []
    for group in range(kv_heads):
        low = group * HD
        high = low + HD
        key_acc = jnp.zeros((length, HD), jnp.float32)
        value_acc = jnp.zeros((length, HD), jnp.float32)
        for number, first in enumerate(starts):
            last = first + block
            query_pos = first + jnp.arange(block)[:, None]
            key_pos = jnp.arange(last)[None, :]
            allowed = key_pos <= query_pos
            key_block = head_k[:last, low:high]
            value_block = head_v[:last, low:high]
            for member in range(groups):
                head = group * groups + member
                query_block = head_q[first:last, head * HD : (head + 1) * HD]
                grad_block = head_g[first:last, head * HD : (head + 1) * HD]
                scores = (
                    lax.dot_general(
                        query_block,
                        key_block,
                        (((1,), (1,)), ((), ())),
                        preferred_element_type=jnp.float32,
                    )
                    * scale
                )
                scores = jnp.where(allowed, scores, -jnp.inf)
                top = jnp.max(scores, axis=1, keepdims=True)
                expo = jnp.where(allowed, jnp.exp(scores - top), 0.0)
                probs = expo / jnp.sum(expo, axis=1, keepdims=True)
                probs_b = probs.astype(jnp.bfloat16)
                value_acc = value_acc.at[:last].add(
                    lax.dot_general(
                        probs_b,
                        grad_block,
                        (((0,), (0,)), ((), ())),
                        preferred_element_type=jnp.float32,
                    )
                )
                prob_grad = lax.dot_general(
                    grad_block,
                    value_block,
                    (((1,), (1,)), ((), ())),
                    preferred_element_type=jnp.float32,
                )
                delta = jnp.sum(probs * prob_grad, axis=1, keepdims=True)
                score_grad = (probs * (prob_grad - delta) * scale).astype(jnp.bfloat16)
                query_parts[number][head] = jnp.dot(
                    score_grad, key_block, preferred_element_type=jnp.float32
                ).astype(jnp.bfloat16)
                key_acc = key_acc.at[:last].add(
                    lax.dot_general(
                        score_grad,
                        query_block,
                        (((0,), (0,)), ((), ())),
                        preferred_element_type=jnp.float32,
                    )
                )
        key_groups.append(key_acc)
        value_groups.append(value_acc)
    head_query_grad = jnp.concatenate(
        [jnp.concatenate(parts, axis=1) for parts in query_parts], axis=0
    )
    rows_pos = jnp.arange(length)
    key_total = jnp.stack(key_groups, axis=1)
    key_grad = unrotate(key_total, rows_pos).reshape(length, kv_heads * HD).astype(jnp.bfloat16)
    value_grad = jnp.concatenate(value_groups, axis=1).astype(jnp.bfloat16)
    query_grad = lax.all_to_all(head_query_grad, "seq", split_axis=0, concat_axis=1, tiled=True)
    width = normed.shape[1]
    piece = lax.all_gather(normed, "seq", axis=0, tiled=True)
    key_part = lax.dot_general(
        piece, key_grad, (((0,), (0,)), ((), ())), preferred_element_type=jnp.float32
    )
    value_part = lax.dot_general(
        piece, value_grad, (((0,), (0,)), ((), ())), preferred_element_type=jnp.float32
    )
    key_full, value_full = lax.psum((key_part, value_part), "dp")
    share = width // lax.axis_size("dp")
    offset = lax.axis_index("dp") * share
    key_weight_grad = lax.dynamic_slice_in_dim(key_full, offset, share, 0)
    value_weight_grad = lax.dynamic_slice_in_dim(value_full, offset, share, 0)
    return (query_grad, key_weight_grad, value_weight_grad)


CORE, XBIT, ZLOW, ZHIGH = 1, 2, 4, 8


def flip(array, mask):
    return lax.ppermute(array, "dp", [(i, i ^ mask) for i in range(16)])


def swap_seq(array):
    return lax.ppermute(array, "seq", [(0, 1), (1, 0)])


def params(limit=VMEM_LIMIT):
    return pltpu.CompilerParams(vmem_limit_bytes=limit)


def vmem():
    return pl.BlockSpec(memory_space=pltpu.VMEM)


def smem():
    return pl.BlockSpec(memory_space=pltpu.SMEM)


def rotary_tables(length):
    half = HD // 2
    freqs = np.exp(-math.log(500000.0) * (2.0 * np.arange(half, dtype=np.float64) / HD))
    angle = np.arange(length, dtype=np.float64)[:, None] * freqs[None, :]
    cosine = np.concatenate([np.cos(angle), np.cos(angle)], axis=1)
    sine = np.concatenate([np.sin(angle), -np.sin(angle)], axis=1)
    return cosine.astype(np.float32), sine.astype(np.float32)


def hbm():
    return pl.BlockSpec(memory_space=pltpu.HBM)


def in_hbm(array):
    return pltpu.with_memory_space_constraint(array, pltpu.HBM)


def run_copies(copies):
    for copy in copies:
        copy.start()
    for copy in copies:
        copy.wait()


def prepare_kv(keys, values):
    rows, kv_width = keys.shape
    wide = kv_width // (2 * NC)

    def body(k_hbm, v_hbm, k_ref, v_ref, *rest):
        kv, sem = rest[:NC], rest[NC]
        run_copies(
            [
                pltpu.make_async_copy(k_hbm, k_ref, sem.at[0]),
                pltpu.make_async_copy(v_hbm, v_ref, sem.at[1]),
            ]
        )
        for chunk, out in enumerate(kv):
            for number, ref in enumerate((k_ref, v_ref)):
                for half in range(2):
                    low = (half * NC + chunk) * wide
                    at = (number * 2 + half) * wide
                    out[:, at : at + wide] = ref[:, low : low + wide]

    return pl.pallas_call(
        body,
        out_shape=[pltpu.VMEM((rows, kv_width), BF)] * 2 + [pltpu.VMEM((rows, 4 * wide), BF)] * NC,
        in_specs=[hbm()] * 2,
        out_specs=[vmem()] * (2 + NC),
        scratch_shapes=[pltpu.SemaphoreType.DMA((2,))],
        compiler_params=params(),
        name="prepare_kv",
    )(in_hbm(keys), in_hbm(values))


def prepare_normed(normed, me, after):
    rows, width = normed.shape
    share = width // 16

    def body(me_ref, x_hbm, after_ref, *rest):
        parts, (x_ref, sem) = rest[:4], rest[4:]
        mine = me_ref[0]
        run_copies([pltpu.make_async_copy(x_hbm, x_ref, sem)])
        for place, part in enumerate(parts):
            for number, mask in enumerate((ZHIGH, ZHIGH | CORE, 0, CORE)):
                low = pl.multiple_of((mine ^ (mask | (place * 2))) * share, share)
                part[number] = x_ref[:, pl.ds(low, share)]

    return pl.pallas_call(
        body,
        out_shape=[pltpu.VMEM((4, rows, share), BF)] * 4,
        in_specs=[smem(), hbm(), hbm()],
        out_specs=[vmem()] * 4,
        scratch_shapes=[pltpu.VMEM((rows, width), BF), pltpu.SemaphoreType.DMA],
        compiler_params=params(),
        name="prepare_normed",
    )(me, in_hbm(normed), after)


def stage(arrays):
    count = len(arrays)

    def body(*refs):
        run_copies(
            [
                pltpu.make_async_copy(refs[n], refs[count + n], refs[-1].at[n])
                for n in range(count)
            ]
        )

    return pl.pallas_call(
        body,
        out_shape=[pltpu.VMEM(one.shape, one.dtype) for one in arrays],
        in_specs=[hbm()] * count,
        out_specs=[vmem()] * count,
        scratch_shapes=[pltpu.SemaphoreType.DMA((count,))],
        compiler_params=params(),
        name="stage",
    )(*[in_hbm(one) for one in arrays])


def join_cores(same, recv, after):
    def body(a_ref, b_ref, *refs):
        out = refs[-1]
        for place in range(4):
            out[place, 0] = a_ref[place]
            out[place, 1] = b_ref[place]

    return pl.pallas_call(
        body,
        out_shape=pltpu.VMEM((4, 2) + same.shape[1:], BF),
        in_specs=[vmem()] * 2 + [hbm()] * len(after),
        out_specs=vmem(),
        compiler_params=params(),
        name="join_cores",
    )(same, recv, *after)


def pack_normed(parts, numbers, after):
    rows, share = parts[0].shape[1:]
    shapes = [(4,) + (len(group),) * (len(group) > 1) + (rows, share) for group in numbers]

    def body(*refs):
        for group, out in zip(numbers, refs[-len(numbers) :]):
            for place in range(4):
                if len(group) > 1:
                    for at, number in enumerate(group):
                        out[place, at] = refs[place][number]
                else:
                    out[place] = refs[place][group[0]]

    return pl.pallas_call(
        body,
        out_shape=[pltpu.VMEM(shape, BF) for shape in shapes],
        in_specs=[vmem()] * 4 + [hbm()] * len(after),
        out_specs=[vmem()] * len(shapes),
        compiler_params=params(),
        name="pack_normed",
    )(*parts, *after)


def combine(seq_at, keep_a, keep_b, recv, after):
    rows, wide = keep_a.shape

    def body(at_ref, a_ref, b_ref, recv_ref, *rest):
        out = rest[-1]
        early = (a_ref[...] + recv_ref[:rows].astype(F32)).astype(BF)

        @pl.when(at_ref[0] == 0)
        def _():
            out[:rows] = early
            out[rows:] = recv_ref[rows:]

        @pl.when(at_ref[0] == 1)
        def _():
            out[:rows] = b_ref[...]
            out[rows:] = early

    return pl.pallas_call(
        body,
        out_shape=jax.ShapeDtypeStruct((2 * rows, wide), BF),
        in_specs=[smem(), vmem(), vmem(), vmem()] + [hbm()] * len(after),
        out_specs=vmem(),
        compiler_params=params(),
        name="combine",
    )(seq_at, keep_a, keep_b, recv, *after)


def attention(
    chunk, seq_at, queries, out_grad, keys, values, kv_recv, cosine, sine, after
):
    rows, width = queries.shape
    wide = width // (2 * NC)
    kv_wide = keys.shape[1] // (2 * NC)
    kv_heads = kv_wide // HD
    groups = wide // kv_wide
    span = groups * rows
    scale = 1.0 / math.sqrt(HD)

    def rotate(grad, cos, sin):
        return grad * cos + pltpu.roll(grad, HD // 2, 1) * sin

    def nt(a, b):
        return lax.dot_general(a, b, (((1,), (1,)), ((), ())), preferred_element_type=F32)

    def tn(a, b):
        return lax.dot_general(a, b, (((0,), (0,)), ((), ())), preferred_element_type=F32)

    def body(at_ref, q_ref, g_ref, k_ref, v_ref, kv_ref, cos_ref, sin_ref, *rest):
        qg_ref, keep_a, keep_b, send = rest[-4:]
        late = at_ref[0]

        def columns(j, size):
            return pl.ds(pl.multiple_of(((late ^ j) * NC + chunk) * size, size), size)

        for j in (1, 0):
            one_side(
                j, late,
                q_ref.at[:, columns(j, wide)], g_ref.at[:, columns(j, wide)],
                k_ref.at[:, columns(j, kv_wide)], v_ref.at[:, columns(j, kv_wide)],
                kv_ref, cos_ref, sin_ref, qg_ref.at[j], keep_a, keep_b, send,
            )

    def one_side(
        other, late, q_ref, g_ref, k_ref, v_ref, kv_ref, cos_ref, sin_ref, qg_ref, keep_a, keep_b, send
    ):
        def earlier(number, head):
            low = (number * 2 + (late ^ other)) * kv_wide + head * HD
            return kv_ref[:, pl.ds(pl.multiple_of(low, HD), HD)]

        def stack(ref, head):
            return jnp.concatenate(
                [
                    ref[:, (head * groups + m) * HD : (head * groups + m + 1) * HD]
                    for m in range(groups)
                ],
                axis=0,
            )

        def one_head(head, is_late):
            cols = slice(head * HD, (head + 1) * HD)
            qs = stack(q_ref, head)
            gs = stack(g_ref, head)
            ks = k_ref[:, cols]
            vs = v_ref[:, cols]
            if is_late:
                ks = jnp.concatenate([earlier(0, head), ks], axis=0)
                vs = jnp.concatenate([earlier(1, head), vs], axis=0)
            count = ks.shape[0]
            scores = nt(ks, qs)
            key_pos = lax.broadcasted_iota(jnp.int32, (rows, span), 0)
            query_pos = lax.broadcasted_iota(jnp.int32, (rows, span), 1) % rows
            diagonal = jnp.where(key_pos <= query_pos, scores[count - rows :], -1e30)
            scores = jnp.concatenate([scores[:rows], diagonal], axis=0) if is_late else diagonal
            top = jnp.max(scores, axis=0, keepdims=True)
            expo = jnp.exp2((scores - top) * (scale / math.log(2.0)))
            probs = expo * (1.0 / jnp.sum(expo, axis=0, keepdims=True))
            value_grad = jnp.dot(probs.astype(BF), gs, preferred_element_type=F32)
            prob_grad = nt(vs, gs)
            delta = jnp.sum(probs * prob_grad, axis=0, keepdims=True)
            score_grad = (probs * (prob_grad - delta) * scale).astype(BF)
            key_grad = jnp.dot(score_grad, qs, preferred_element_type=F32)
            query_grad = tn(score_grad, ks).astype(BF)
            for m in range(groups):
                low = (head * groups + m) * HD
                qg_ref[:, low : low + HD] = query_grad[m * rows : (m + 1) * rows]
            first = (rotate(key_grad[:rows], cos_ref[:rows], sin_ref[:rows]), value_grad[:rows])
            second = None
            if is_late:
                second = (
                    rotate(key_grad[rows:], cos_ref[rows:], sin_ref[rows:]),
                    value_grad[rows:],
                )
            return first, second

        def all_heads(is_late):
            parts = [one_head(head, is_late) for head in range(kv_heads)]

            def write(first_ref, second_ref, second_at):
                for head, (first, second) in enumerate(parts):
                    for number in range(2):
                        at = slice(number * kv_wide + head * HD, number * kv_wide + (head + 1) * HD)
                        first_ref[:rows, at] = first[number].astype(first_ref.dtype)
                        later = jnp.zeros((rows, HD), BF) if second is None else second[number].astype(BF)
                        second_ref[second_at : second_at + rows, at] = later

            if other == 0:
                write(keep_a, keep_b, 0)
            else:
                write(send, send, rows)

        @pl.when(late == 1)
        def _():
            all_heads(True)

        @pl.when(late == 0)
        def _():
            all_heads(False)

    operands = [seq_at, queries, out_grad, keys, values, kv_recv, cosine, sine]
    return pl.pallas_call(
        body,
        out_shape=[
            pltpu.VMEM((2, rows, wide), BF),
            pltpu.VMEM((rows, 2 * kv_wide), F32),
            pltpu.VMEM((rows, 2 * kv_wide), BF),
            pltpu.VMEM((2 * rows, 2 * kv_wide), BF),
        ],
        in_specs=[smem()] + [vmem()] * 7 + [hbm()] * len(after),
        out_specs=[vmem()] * 4,
        compiler_params=params(),
        name="attention",
    )(*operands, *after)


def tn(a, b):
    return lax.dot_general(a, b, (((0,), (0,)), ((), ())), preferred_element_type=F32)


def project_away(normed_own, normed_other, grads, after):
    share = normed_own.shape[3]
    wide = grads[0].shape[1]

    def body(xa_ref, xb_ref, *refs):
        ys, keep, sends = refs[:4], refs[-1 - CUT], refs[-CUT:]
        right = jnp.concatenate([ref[...] for ref in ys], axis=0)

        def total(core):
            left = [x_ref[place, core] for place in range(4) for x_ref in (xa_ref, xb_ref)]
            return tn(jnp.concatenate(left, axis=0), right)

        keep[...] = total(0)
        sent = total(1)
        for n, out in enumerate(sends):
            out[...] = sent[n * share // CUT : (n + 1) * share // CUT]

    return pl.pallas_call(
        body,
        out_shape=[pltpu.VMEM((share, wide), F32)] + [pltpu.VMEM((share // CUT, wide), F32)] * CUT,
        in_specs=[vmem()] * 6 + [hbm()] * len(after),
        out_specs=[vmem()] * (1 + CUT),
        compiler_params=params(),
        name="project_away",
    )(normed_own, normed_other, *grads, *after)


def add_round(own, recv, after):
    rows = own.shape[0] // CUT

    def body(a_ref, *refs):
        out = refs[-1]
        for n, b_ref in enumerate(refs[:CUT]):
            at = slice(n * rows, (n + 1) * rows)
            out[at] = (a_ref[at] + b_ref[...]).astype(BF)

    return pl.pallas_call(
        body,
        out_shape=pltpu.VMEM(own.shape, BF),
        in_specs=[vmem()] * (1 + CUT) + [hbm()] * len(after),
        out_specs=vmem(),
        compiler_params=params(),
        name="add_round",
    )(own, *recv, *after)


def join_places(grads, after):
    length, wide = grads[0].shape

    def body(*refs):
        out = refs[-1]
        for place, ref in enumerate(refs[:4]):
            out[place * length : (place + 1) * length] = ref[...]

    return pl.pallas_call(
        body,
        out_shape=pltpu.VMEM((4 * length, wide), BF),
        in_specs=[vmem()] * 4 + [hbm()] * len(after),
        out_specs=vmem(),
        compiler_params=params(),
        name="join_places",
    )(*grads, *after)


def project_home(seq_at, normed, grads, recv, query_grads, halves, after):
    rows, share = normed[0].shape[2:]
    wide = grads[0][0].shape[1]
    chunks = len(grads)
    part = query_grads[0].shape[2]
    ready = len(halves)
    cols = wide // 2

    def body(at_ref, xa_ref, xb_ref, *refs):
        ys, refs = refs[: 4 * chunks], refs[4 * chunks :]
        others, qs, half_refs = refs[:chunks], refs[chunks : 2 * chunks], refs[2 * chunks : 2 * chunks + ready]
        out, query_out, *outs, sums, sem, sum_sem = refs[-7:]
        copies = []
        for chunk, ref in enumerate(qs):
            for j in range(2):
                low = pl.multiple_of(((at_ref[0] ^ j) * chunks + chunk) * part, part)
                copies.append(
                    pltpu.make_async_copy(ref.at[j], query_out.at[:, pl.ds(low, part)], sem.at[chunk, j])
                )
        for copy in copies:
            copy.start()
        left = [
            x_ref[place, core] for place in range(4) for x_ref in (xa_ref, xb_ref) for core in range(2)
        ]
        left = jnp.concatenate(left, axis=0)
        for chunk in range(chunks):
            right = []
            for place in range(4):
                for seq in range(2):
                    right.append(ys[chunk * 4 + place][seq * rows : (seq + 1) * rows, :])
                    low = (place * 2 + seq) * rows
                    right.append(others[chunk][low : low + rows, :])
            total = tn(left, jnp.concatenate(right, axis=0))
            if chunk >= ready:
                out[:, (chunk - ready) * wide : (chunk - ready + 1) * wide] = total
                continue
            for number in range(2):
                at = slice(number * cols, (number + 1) * cols)
                sums[chunk, number] = total[:, at] + half_refs[chunk][:, at].astype(F32)
                copy = pltpu.make_async_copy(
                    sums.at[chunk, number],
                    outs[number].at[:, chunk * cols : (chunk + 1) * cols],
                    sum_sem.at[chunk, number],
                )
                copy.start()
                copies.append(copy)
        for copy in copies:
            copy.wait()

    return pl.pallas_call(
        body,
        out_shape=[
            pltpu.VMEM((share, (chunks - ready) * wide), F32),
            jax.ShapeDtypeStruct((rows, 2 * chunks * part), BF),
            pltpu.HBM((share, chunks * cols), F32),
            pltpu.HBM((share, chunks * cols), F32),
        ],
        in_specs=[smem()] + [vmem()] * (2 + 6 * chunks + ready) + [hbm()] * len(after),
        out_specs=[vmem(), hbm(), hbm(), hbm()],
        scratch_shapes=[
            pltpu.VMEM((ready, 2, share, cols), F32),
            pltpu.SemaphoreType.DMA((chunks, 2)),
            pltpu.SemaphoreType.DMA((ready, 2)),
        ],
        compiler_params=params(),
        name="project_home",
    )(seq_at, *normed, *[part for parts in grads for part in parts], *recv, *query_grads, *halves, *after)


def finish(keep, recv_half, sums):
    rows, wide = keep.shape
    cols = wide // 2
    low = sums[0].shape[1] - cols

    def body(keep_ref, half_ref, *refs):
        outs, total, sem = refs[2:4], refs[4], refs[5]
        copies = []
        for number, out in enumerate(outs):
            at = slice(number * cols, (number + 1) * cols)
            total[number] = keep_ref[:, at] + half_ref[:, at].astype(F32)
            copies.append(
                pltpu.make_async_copy(total.at[number], out.at[:, low : low + cols], sem.at[number])
            )
            copies[-1].start()
        for copy in copies:
            copy.wait()

    return pl.pallas_call(
        body,
        out_shape=[pltpu.HBM(one.shape, F32) for one in sums],
        in_specs=[vmem()] * 2 + [hbm()] * 2,
        out_specs=[hbm()] * 2,
        scratch_shapes=[pltpu.VMEM((2, rows, cols), F32), pltpu.SemaphoreType.DMA((2,))],
        input_output_aliases={2: 0, 3: 1},
        compiler_params=params(),
        name="finish",
    )(keep, recv_half, *[in_hbm(one) for one in sums])


def cube_local(queries, keys, values, out_grad, normed):
    seq_at = jnp.reshape(lax.axis_index("seq"), (1,)).astype(jnp.int32)
    me = jnp.reshape(lax.axis_index("dp"), (1,)).astype(jnp.int32)
    rows = queries.shape[0]
    cosine, sine = (jnp.asarray(table) for table in rotary_tables(2 * rows))

    keys, values, *kv = prepare_kv(keys, values)
    parts = prepare_normed(normed, me, kv[0])
    kv_recv = [lax.ppermute(part, "seq", [(0, 1)]) for part in kv]
    masks = (0, XBIT, ZLOW, XBIT | ZLOW)
    parts = [flip(part, mask) if mask else part for part, mask in zip(parts, masks)]
    q_in, g_in, cosine, sine = stage([queries, out_grad, cosine, sine])

    query_grads, made = [], []
    for chunk in range(NC):
        query_grad, *rest = attention(
            chunk, seq_at, q_in, g_in, keys, values, kv_recv[chunk], cosine, sine,
            [parts[1], parts[3]] + query_grads if chunk else [],
        )
        query_grads.append(query_grad)
        made.append(rest)

    grads = []
    after = [made[-1][0]]
    for keep_a, keep_b, send in made:
        mine = combine(seq_at, keep_a, keep_b, swap_seq(send), after)
        below = flip(mine, ZLOW)
        grads.append([mine, flip(mine, XBIT), below, flip(below, XBIT)])
        after = grads[-1][1:3]

    (away,) = pack_normed(parts, [(0, 1)], [made[-1][0]])
    away_other = swap_seq(away)
    same, cross = pack_normed(parts, [(2,), (3,)], [made[-1][0]])
    cross = flip(cross, CORE)

    recv_half, recv_core = [], []
    home = join_cores(same, cross, [away_other])
    home_other = swap_seq(home)
    after, fence = [grads[1][2], cross], [grads[1][1], home]
    for part in grads:
        own, *sends = project_away(away, away_other, part, after)
        total = add_round(own, [flip(send, CORE) for send in sends], fence)
        gathered = join_places(part, [total] + recv_half)
        recv_core.append(flip(gathered, CORE))
        recv_half.append(flip(total, ZHIGH))
        if part is grads[0]:
            after, fence = recv_core[:], [home_other]
    keep, query_grad, *sums = project_home(
        seq_at, (home, home_other), grads, recv_core, query_grads, recv_half[:-1], [total]
    )
    key_weight_grad, value_weight_grad = finish(keep, recv_half[-1], sums)
    return (query_grad, key_weight_grad, value_weight_grad)


def solution(mesh):
    spread = P(("dp", "seq"), None)
    cube = dict(mesh.shape) == {"dp": 16, "seq": 2}
    return jax.shard_map(
        cube_local if cube else general_local,
        mesh=mesh,
        in_specs=(spread,) * 5,
        out_specs=(spread, P("dp", "seq"), P("dp", "seq")),
        check_vma=False,
    )
```
